256 devices in a mesh: gz: 256 (over y, x, z, core).
Axes of the slice: x: 4, y: 4, z: 8, core: 2. Of those that a mesh axis runs over, the one named last changes fastest.
Arguments:
- tokens: bfloat16 [256, 64, 128, 128], P('gz'), may hold values from -64 to 64
- cotangent: bfloat16 [256, 64, 128, 128], P('gz'), may hold values from -24 to 24
- w_query: bfloat16 [128, 128], replicated, may hold values from -1 to 1
- w_key: bfloat16 [128, 128], replicated, may hold values from -0.5 to 0.5
- w_value: bfloat16 [128, 128], replicated, may hold values from -0.5 to 0.5
- w_out: bfloat16 [128, 128], replicated, may hold values from -0.5 to 0.5
- ln_gain: float32 [128], replicated, may hold values from 0.5 to 1.5
- ln_bias: float32 [128], replicated, may hold values from -1 to 1
Outputs:
- d_tokens: bfloat16 [256, 64, 128, 128], P('gz')
- d_query: float32 [128, 128], replicated
- d_out: float32 [128, 128], replicated
- d_key: float32 [128, 128], replicated
- d_value: float32 [128, 128], replicated
- d_gain: float32 [128], replicated
- d_bias: float32 [128], replicated
- pooled_grad: float32 [512, 128], replicated
The draws below stay inside these ranges and needn't reach their ends.
All inputs are finite; a program needn't handle non-finite values.
Results may differ from the reference program's by a relative error of at most 0.023.
The reference program's roundings to bfloat16 on the way count: a program that leaves them out, or rounds other values in their place, can miss the bound.
Values sent between devices are 32-bit elements; how exact they have to be, the bound alone decides.
A program may use at most 64 MiB of HBM per device.

```python
import jax
import jax.numpy as jnp
from jax import lax

D = 128
HEADS = 4
POOL = 16
PLANE_X = 128
ROWS_Y = 64
SLABS = 256


def draw_tokens(key, part):
    key = jax.random.fold_in(key, 11)
    shape = (SLABS, ROWS_Y, PLANE_X, D)
    return jnp.clip(jax.random.normal(key, shape, jnp.float32), -6.0, 6.0).astype(jnp.bfloat16)


def draw_w_query(key, part):
    key = jax.random.fold_in(key, 23)
    normal_part = jnp.clip(jax.random.normal(key, (D, D), jnp.float32), -4.0, 4.0) * D ** (-0.5)
    return jnp.clip(normal_part, -1.0, 1.0).astype(jnp.bfloat16)


def levels(rng, dims, cuts, low, largest):
    loudness = 1.0
    for position, blocks in cuts:
        steps = jax.random.uniform(jax.random.fold_in(jax.random.fold_in(rng, 6), position), (blocks,), jnp.float32, low / len(cuts), largest / len(cuts))
        loudness = loudness * jnp.repeat(jnp.exp(steps), dims[position] // blocks).reshape((-1,) + (1,) * (len(dims) - 1 - position))
    return loudness


def normal_values(rng, dims, deviation, bound, shards=(), kind=jnp.bfloat16):
    drawn = deviation * jax.random.normal(rng, dims, jnp.float32)
    if shards:
        drawn = drawn * levels(rng, dims, shards, -0.22, 0.18)
    return jnp.clip(drawn, -bound, bound).astype(kind)


def setup_inputs(seed: int = 0) -> dict:
    arg_keys = jax.random.split(jax.random.key(seed), 9)
    return {
        "tokens": draw_tokens(jax.random.fold_in(arg_keys[8], 71), 0),
        "cotangent": normal_values(arg_keys[1], (SLABS, ROWS_Y, PLANE_X, D), 4.0, 24.0, ((0, 256),)),
        "w_query": draw_w_query(jax.random.fold_in(arg_keys[8], 71), 0),
        "w_key": normal_values(arg_keys[3], (D, D), D ** -0.5, 0.5),
        "w_value": normal_values(arg_keys[4], (D, D), D ** -0.5, 0.5),
        "w_out": normal_values(arg_keys[5], (D, D), D ** -0.5, 0.5),
        "ln_gain": jnp.clip(1.0 + 0.1 * jax.random.normal(arg_keys[6], (D,), jnp.float32), 0.5, 1.5),
        "ln_bias": jnp.clip(jax.random.uniform(arg_keys[7], (D,), jnp.float32, -1.0, 1.0), -1.0, 1.0),
    }


EPSILON = 1e-05

def layer_norm_rows(pooled, ln_gain, ln_bias):
    row_mean = lax.optimization_barrier(jnp.mean(pooled, axis=1, keepdims=True))
    centered = pooled - row_mean
    row_var = lax.optimization_barrier(jnp.mean(centered * centered, axis=1, keepdims=True))
    inv_std = lax.rsqrt(row_var + EPSILON)
    standard = centered * inv_std
    return (standard, inv_std, standard * ln_gain + ln_bias)

def key_backward(key_grads, value_grads, standard, inv_std, normed_low, w_key, w_value, ln_gain):
    normed_wide = normed_low.astype(jnp.float32)
    grad_key = jnp.einsum('kd,ke->de', normed_wide, key_grads, precision=lax.Precision.HIGHEST)
    grad_value = jnp.einsum('kd,ke->de', normed_wide, value_grads, precision=lax.Precision.HIGHEST)
    key_low = key_grads.astype(jnp.bfloat16)
    value_low = value_grads.astype(jnp.bfloat16)
    d_normed = jnp.dot(key_low, w_key.T, preferred_element_type=jnp.float32) + jnp.dot(value_low, w_value.T, preferred_element_type=jnp.float32)
    grad_gain = lax.optimization_barrier(jnp.sum(d_normed * standard, axis=0))
    grad_bias = lax.optimization_barrier(jnp.sum(d_normed, axis=0))
    scaled = d_normed * ln_gain
    d_pooled = inv_std * (scaled - lax.optimization_barrier(jnp.mean(scaled, axis=1, keepdims=True)) - standard * lax.optimization_barrier(jnp.mean(scaled * standard, axis=1, keepdims=True)))
    return (d_pooled, grad_key, grad_value, grad_gain, grad_bias)

def attend_block(query_rows, grad_rows, w_query, w_out, key_heads, value_heads, score_scale):
    block_rows, features = query_rows.shape
    head_dim = features // HEADS
    query_low = jnp.dot(query_rows, w_query, preferred_element_type=jnp.float32).astype(jnp.bfloat16)
    query_heads = query_low.reshape(block_rows, HEADS, head_dim).astype(jnp.float32)
    keys_wide = key_heads.astype(jnp.float32)
    values_wide = value_heads.astype(jnp.float32)
    scores = jnp.einsum('qhe,khe->hqk', query_heads, keys_wide) * score_scale
    row_max = lax.optimization_barrier(jnp.max(scores, axis=2, keepdims=True))
    exponent = jnp.exp(scores - row_max)
    attention = exponent / lax.optimization_barrier(jnp.sum(exponent, axis=2, keepdims=True))
    attention_low = attention.astype(jnp.bfloat16)
    attn_low = jnp.einsum('hqk,khe->qhe', attention_low.astype(jnp.float32), values_wide).reshape(block_rows, features).astype(jnp.bfloat16)
    out_part = jnp.einsum('qd,qe->de', attn_low.astype(jnp.float32), grad_rows.astype(jnp.float32))
    d_attn_low = jnp.dot(grad_rows, w_out.T, preferred_element_type=jnp.float32).astype(jnp.bfloat16)
    d_heads = d_attn_low.reshape(block_rows, HEADS, head_dim).astype(jnp.float32)
    d_probs = jnp.einsum('qhe,khe->hqk', d_heads, values_wide)
    row_delta = lax.optimization_barrier(jnp.sum(attention * d_probs, axis=2, keepdims=True))
    d_scores_low = (attention * (d_probs - row_delta) * score_scale).astype(jnp.bfloat16)
    value_part = jnp.einsum('hqk,qhe->khe', attention_low.astype(jnp.float32), d_heads)
    key_part = jnp.einsum('hqk,qhe->khe', d_scores_low.astype(jnp.float32), query_heads)
    dq_low = jnp.einsum('hqk,khe->qhe', d_scores_low.astype(jnp.float32), keys_wide).reshape(block_rows, features).astype(jnp.bfloat16)
    query_part = jnp.einsum('qd,qe->de', query_rows.astype(jnp.float32), dq_low.astype(jnp.float32))
    return (dq_low, key_part, value_part, query_part, out_part)

def reference(tokens, cotangent, w_query, w_key, w_value, w_out, ln_gain, ln_bias):
    slabs, rows_y, plane_x, features = tokens.shape
    cells_y = rows_y // POOL
    cells_x = plane_x // POOL
    cells_dev = cells_y * cells_x
    key_count = cells_dev * slabs // POOL
    head_dim = features // HEADS
    score_scale = head_dim ** (-0.5)

    def pool_slab(slab_tokens):
        return lax.optimization_barrier(jnp.sum(slab_tokens.astype(jnp.float32).reshape(cells_y, POOL, cells_x, POOL, features), axis=(1, 3)))
    parts = lax.map(pool_slab, tokens)
    parts = lax.optimization_barrier(jnp.sum(parts.reshape(slabs // (2 * POOL), POOL, 2, cells_y, cells_x, features), axis=1))
    pooled = parts.reshape(key_count, features) / float(POOL ** 3)
    standard, inv_std, normed = layer_norm_rows(pooled, ln_gain, ln_bias)
    normed_low = normed.astype(jnp.bfloat16)
    key_rows = jnp.dot(normed_low, w_key, preferred_element_type=jnp.float32).astype(jnp.bfloat16)
    value_rows = jnp.dot(normed_low, w_value, preferred_element_type=jnp.float32).astype(jnp.bfloat16)
    key_heads = key_rows.reshape(key_count, HEADS, head_dim)
    value_heads = value_rows.reshape(key_count, HEADS, head_dim)
    slab_rows = rows_y * plane_x
    block_rows = min(512, slab_rows)
    block_count = slab_rows // block_rows
    zero_keys = jnp.zeros((key_count, HEADS, head_dim), jnp.float32)
    zero_square = jnp.zeros((features, features), jnp.float32)

    def per_block(running, inputs):
        query_rows, grad_rows = inputs
        dq_low, key_part, value_part, query_part, out_part = attend_block(query_rows, grad_rows, w_query, w_out, key_heads, value_heads, score_scale)
        return ((running[0] + key_part, running[1] + value_part, running[2] + query_part, running[3] + out_part), dq_low)

    def per_slab(running, inputs):
        slab_tokens, slab_grads = inputs
        query_blocks = slab_tokens.reshape(block_count, block_rows, features)
        grad_blocks = slab_grads.reshape(block_count, block_rows, features)
        running, dq_blocks = lax.scan(per_block, running, (query_blocks, grad_blocks))
        return (running, dq_blocks.reshape(slab_rows, features))
    totals, dq_all = lax.scan(per_slab, (zero_keys, zero_keys, zero_square, zero_square), (tokens, cotangent))
    key_grads = totals[0].reshape(key_count, features)
    value_grads = totals[1].reshape(key_count, features)
    d_pooled, grad_key, grad_value, grad_gain, grad_bias = key_backward(key_grads, value_grads, standard, inv_std, normed_low, w_key, w_value, ln_gain)

    def slab_input_grad(inputs):
        slab_number, dq_low = inputs
        offset = (slab_number // (2 * POOL) * 2 + slab_number % 2) * cells_dev
        own_rows = lax.dynamic_slice_in_dim(d_pooled, offset.astype(jnp.int32), cells_dev, 0) / float(POOL ** 3)
        spread = jnp.broadcast_to(own_rows.reshape(cells_y, 1, cells_x, 1, features), (cells_y, POOL, cells_x, POOL, features)).reshape(slab_rows, features)
        summed = jnp.dot(dq_low, w_query.T, preferred_element_type=jnp.float32) + spread
        return summed.astype(jnp.bfloat16).reshape(rows_y, plane_x, features)
    d_tokens = lax.map(slab_input_grad, (jnp.arange(slabs, dtype=jnp.int32), dq_all))
    grad_scale = float(slabs * slab_rows) ** (-0.5)
    return (d_tokens, totals[2] * grad_scale, totals[3] * grad_scale, grad_key * grad_scale, grad_value * grad_scale, grad_gain * grad_scale, grad_bias * grad_scale, d_pooled * grad_scale)
```

```python
import functools
import math

import jax
import jax.numpy as jnp
from jax import lax
from jax.experimental import pallas as pl
from jax.experimental.pallas import tpu as pltpu
from jax.sharding import PartitionSpec as P

HEADS = 4
POOL = 16
EPSILON = 1e-05
MESH = pl.DeviceIdType.MESH
F32 = jnp.float32
BF16 = jnp.bfloat16

Z = 8
PLANE = 16
QUERIES = 256
KEY_CHUNK = 128
SAFE_LOG2 = 60.0


def dot(a, b):
    return lax.dot_general(a, b, (((1,), (0,)), ((), ())), preferred_element_type=F32)


def dot_nt(a, b):
    return lax.dot_general(a, b, (((1,), (1,)), ((), ())), preferred_element_type=F32)


def greet(partners):
    barrier = pltpu.get_barrier_semaphore()
    for partner in partners:
        pl.semaphore_signal(barrier, inc=1, device_id=(partner,), device_id_type=MESH)
    pl.semaphore_wait(barrier, len(partners))


def send(src, dst, send_sem, recv_sem, partner):
    copy = pltpu.make_async_remote_copy(
        src_ref=src,
        dst_ref=dst,
        send_sem=send_sem,
        recv_sem=recv_sem,
        device_id=(partner,),
        device_id_type=MESH,
    )
    copy.start()
    return copy


def pool_kernel(part_ref, out_ref, near, far, near_send, near_recv, far_send, far_recv):
    me = lax.axis_index("gz")
    core, chip = lax.rem(me, 2), me // 2
    member, block = lax.rem(chip, 16), chip // 16
    group = block * 2 + core
    near_ids, far_ids = [], []
    for t in range(1, 16):
        near_ids.append((block * 16 + lax.rem(member + t, 16)) * 2 + core)
        other = lax.rem(group + t, 16)
        far_ids.append(((other // 2) * 16 + member) * 2 + lax.rem(other, 2))
    greet(near_ids + far_ids)
    copies = [
        send(part_ref, near.at[member], near_send.at[t], near_recv.at[t], near_ids[t])
        for t in range(15)
    ]
    near[member] = part_ref[...]
    for copy in copies:
        copy.wait()
    total = near[0]
    for m in range(1, 16):
        total = total + near[m]
    far[group] = total
    copies = [
        send(far.at[group], far.at[group], far_send.at[t], far_recv.at[t], far_ids[t])
        for t in range(15)
    ]
    for copy in copies:
        copy.wait()
    for g in range(16):
        out_ref[pl.ds(g * 32, 32), :] = far[g]


def exchange_pools(part):
    rows, features = part.shape
    return pl.pallas_call(
        pool_kernel,
        name="pool_exchange",
        out_shape=jax.ShapeDtypeStruct((16 * rows, features), F32),
        in_specs=[pl.BlockSpec(memory_space=pltpu.VMEM)],
        out_specs=pl.BlockSpec(memory_space=pltpu.VMEM),
        scratch_shapes=[
            pltpu.VMEM((16, rows, features), F32),
            pltpu.VMEM((16, rows, features), F32),
            pltpu.SemaphoreType.DMA((15,)),
            pltpu.SemaphoreType.DMA((15,)),
            pltpu.SemaphoreType.DMA((15,)),
            pltpu.SemaphoreType.DMA((15,)),
        ],
        compiler_params=pltpu.CompilerParams(collective_id=0, has_side_effects=True),
    )(part)


def sum_kernel(
    w_ref, out_ref, got_half, half, got, along, full, pair_send, pair_recv, sum_send, sum_recv,
    z_send, z_recv, all_send, all_recv,
):
    me = lax.axis_index("gz")
    core, chip = lax.rem(me, 2), me // 2
    z, plane = lax.rem(chip, Z), chip // Z
    half_rows = half.shape[0]
    share = half_rows // PLANE
    sibling = me + 1 - 2 * core
    plane_members = [lax.rem(plane + t, PLANE) for t in range(1, PLANE)]
    plane_ids = [(other * Z + z) * 2 + core for other in plane_members]
    z_ids = [(plane * Z + lax.rem(z + t, Z)) * 2 + core for t in range(1, Z)]
    greet([sibling] + plane_ids + z_ids)

    mine = pl.ds(pl.multiple_of(core * half_rows, 8), half_rows)
    theirs = pl.ds(pl.multiple_of((1 - core) * half_rows, 8), half_rows)
    send(w_ref.at[theirs], got_half, pair_send.at[0], pair_recv.at[0], sibling).wait()
    half[...] = w_ref[mine, :] + got_half[...]

    copies = [
        send(
            half.at[pl.ds(pl.multiple_of(plane_members[t] * share, 8), share)],
            got.at[t],
            sum_send.at[t],
            sum_recv.at[t],
            plane_ids[t],
        )
        for t in range(PLANE - 1)
    ]
    total = half[pl.ds(pl.multiple_of(plane * share, 8), share), :]
    for t in range(PLANE - 1):
        copies[t].wait()
        total = total + got[t]

    along[z] = total
    copies = [
        send(along.at[z], along.at[z], z_send.at[t], z_recv.at[t], z_ids[t]) for t in range(Z - 1)
    ]
    for copy in copies:
        copy.wait()
    total = along[0]
    for k in range(1, Z):
        total = total + along[k]
    own = pl.ds(pl.multiple_of(core * half_rows + plane * share, 8), share)
    full[own, :] = total

    copies = [
        send(full.at[own], full.at[own], all_send.at[t], all_recv.at[t], plane_ids[t])
        for t in range(PLANE - 1)
    ]
    for copy in copies:
        copy.wait()
    send(full.at[mine], full.at[mine], pair_send.at[1], pair_recv.at[1], sibling).wait()
    out_ref[...] = full[...]


def sum_devices(w):
    rows, features = w.shape
    share = rows // 2 // PLANE
    dma = pltpu.SemaphoreType.DMA
    return pl.pallas_call(
        sum_kernel,
        name="sum_devices",
        out_shape=jax.ShapeDtypeStruct((rows, features), F32),
        in_specs=[pl.BlockSpec(memory_space=pltpu.VMEM)],
        out_specs=pl.BlockSpec(memory_space=pltpu.VMEM),
        scratch_shapes=[
            pltpu.VMEM((rows // 2, features), F32),
            pltpu.VMEM((rows // 2, features), F32),
            pltpu.VMEM((PLANE - 1, share, features), F32),
            pltpu.VMEM((Z, share, features), F32),
            pltpu.VMEM((rows, features), F32),
            dma((2,)),
            dma((2,)),
            dma((PLANE - 1,)),
            dma((PLANE - 1,)),
            dma((Z - 1,)),
            dma((Z - 1,)),
            dma((PLANE - 1,)),
            dma((PLANE - 1,)),
        ],
        compiler_params=pltpu.CompilerParams(collective_id=1, has_side_effects=True),
    )(w)


def normalise(pool_sums):
    pooled = pool_sums * (1.0 / float(POOL**3))
    mean = jnp.mean(pooled, axis=1, keepdims=True)
    centered = pooled - mean
    var = jnp.mean(centered * centered, axis=1, keepdims=True)
    inv_std = lax.rsqrt(var + EPSILON)
    return centered * inv_std, inv_std


def transposed(w):
    return w.astype(F32).T.astype(BF16)


def three_terms(low, factor, lane_group):
    wide = low.astype(F32) * factor
    high = wide.astype(BF16)
    rest = wide - high.astype(F32)
    middle = rest.astype(BF16)
    last = (rest - middle.astype(F32)).astype(BF16)
    zero = jnp.zeros_like(high)
    return jnp.where(
        lane_group == 0,
        high,
        jnp.where(lane_group == 1, middle, jnp.where(lane_group == 2, last, zero)),
    )


def attend_kernel(
    tokens_ref, cot_ref, pool_ref, w_query_ref, w_key_ref, w_value_ref, w_out_ref, gain_ref,
    bias_ref, sums_ref, dq_ref, q_rows, q_cols, d_rows, d_cols, key_terms, value_terms, key_cols,
    value_cols, exps, dps, probs, dscores,
):
    blocks, queries, features = tokens_ref.shape
    keys = pool_ref.shape[0]
    head_dim = features // HEADS
    scale = head_dim ** (-0.5)
    chunks = keys // KEY_CHUNK

    standard, _ = normalise(pool_ref[...])
    normed_low = (standard * gain_ref[...] + bias_ref[...]).astype(BF16)
    source = lax.broadcasted_iota(jnp.int32, (features, HEADS * features), 0)
    target = lax.broadcasted_iota(jnp.int32, (features, HEADS * features), 1)
    spread = jnp.where(
        source == (target // features) * head_dim + lax.rem(target, head_dim), 1.0, 0.0
    ).astype(BF16)
    lane = lax.broadcasted_iota(jnp.int32, (keys, features), 1)
    lane_group = lane // head_dim
    for w_ref, factor, terms, cols in (
        (w_key_ref, scale * math.log2(math.e), key_terms, key_cols),
        (w_value_ref, scale, value_terms, value_cols),
    ):
        w = w_ref[...]
        wide_w = dot(w, spread).astype(BF16)
        for h in range(HEADS):
            low = dot(normed_low, wide_w[:, h * features : (h + 1) * features]).astype(BF16)
            terms[h] = three_terms(low, factor, lane_group)
        cols[...] = dot_nt(transposed(w), normed_low).astype(BF16)
    key_wide = key_cols[...].astype(F32).reshape(HEADS, head_dim, keys)
    key_norm = jnp.max(jnp.sum(key_wide * key_wide, axis=1), axis=1, keepdims=True)

    w_query = w_query_ref[...]
    w_query_t = transposed(w_query)
    w_out = w_out_ref[...]
    w_out_t = transposed(w_out)

    def project(i, norm):
        rows, grads = tokens_ref[i], cot_ref[i]
        q_rows[i] = dot(rows, w_query).astype(BF16)
        d_rows[i] = dot(grads, w_out_t).astype(BF16)
        cols = dot_nt(w_query_t, rows).astype(BF16)
        q_cols[i] = cols
        d_cols[i] = dot_nt(w_out, grads).astype(BF16)
        wide = cols.astype(F32).reshape(HEADS, head_dim, queries)
        return jnp.maximum(norm, jnp.sum(wide * wide, axis=1))

    norm = lax.fori_loop(0, blocks, project, jnp.zeros((HEADS, queries), F32))
    bound = jnp.max(norm * key_norm) * (scale * math.log2(math.e)) ** 2

    sums_ref[...] = jnp.zeros_like(sums_ref)
    query_head = lax.broadcasted_iota(jnp.int32, (queries, features), 1) // head_dim

    def fold(x):
        return jnp.sum(x.reshape(x.shape[0] // 8, 8, queries), axis=0)

    def first(i, h, slot, safe):
        query = q_cols[i, h * head_dim : (h + 1) * head_dim, :]
        grad = d_cols[i, h * head_dim : (h + 1) * head_dim, :]
        query = jnp.concatenate([query] * HEADS, axis=0)
        grad = jnp.concatenate([grad] * HEADS, axis=0)
        total = jnp.zeros((8, queries), F32)
        delta = jnp.zeros((8, queries), F32)
        if safe:
            top = jnp.full((8, queries), -jnp.inf, F32)
            for c in range(chunks):
                part = pl.ds(c * KEY_CHUNK, KEY_CHUNK)
                s = dot(key_terms[h, part, :], query)
                exps[slot, part, :] = s
                top = jnp.maximum(
                    top, jnp.max(s.reshape(KEY_CHUNK // 8, 8, queries), axis=0)
                )
            top = jnp.max(top, axis=0, keepdims=True)
        for c in range(chunks):
            part = pl.ds(c * KEY_CHUNK, KEY_CHUNK)
            if safe:
                e = jnp.exp2(exps[slot, part, :] - top)
            else:
                e = jnp.exp2(dot(key_terms[h, part, :], query))
            dp = dot(value_terms[h, part, :], grad)
            exps[slot, part, :] = e
            dps[slot, part, :] = dp
            total = total + fold(e)
            delta = delta + fold(e * dp)
        return total, delta

    def second(h, slot, bank, sums):
        total, delta = (jnp.sum(x, axis=0, keepdims=True) for x in sums)
        inverse = 1.0 / total
        delta = delta * inverse
        columns = pl.ds(h * queries, queries)
        for c in range(chunks):
            part = pl.ds(c * KEY_CHUNK, KEY_CHUNK)
            p = exps[slot, part, :] * inverse
            probs[bank, part, columns] = p.astype(BF16)
            dscores[bank, part, columns] = (p * (dps[slot, part, :] - delta)).astype(BF16)
        head = pl.ds(h * head_dim, head_dim)
        attn = dot(value_cols[head, :], probs[bank, :, columns])
        dq = dot(key_cols[head, :], dscores[bank, :, columns])
        return attn, dq

    def third(i, bank, outs):
        attn_low = jnp.concatenate([o[0] for o in outs], axis=0).astype(BF16)
        dq_low = jnp.concatenate([o[1] for o in outs], axis=0).astype(BF16)
        sums_ref[pl.ds(2 * keys, features), :] += dot(dq_low, tokens_ref[i])
        sums_ref[pl.ds(2 * keys + features, features), :] += dot(attn_low, cot_ref[i])
        dq_ref[i] = dq_low.astype(F32).T.astype(BF16)
        zero = jnp.zeros((queries, features), BF16)
        q, d = q_rows[i], d_rows[i]
        q_stack = jnp.concatenate([jnp.where(query_head == h, q, zero) for h in range(HEADS)], 0)
        d_stack = jnp.concatenate([jnp.where(query_head == h, d, zero) for h in range(HEADS)], 0)
        sums_ref[pl.ds(0, keys), :] += dot(dscores[bank], q_stack)
        sums_ref[pl.ds(keys, keys), :] += dot(probs[bank], d_stack)

    def run(at_once, safe):
        def step(j, carry):
            units = [(b, h) for b in range(at_once) for h in range(HEADS)]
            pending = first(j * at_once, 0, 0, safe)
            outs = []
            for n, (b, h) in enumerate(units):
                current = pending
                if n + 1 < len(units):
                    nb, nh = units[n + 1]
                    pending = first(j * at_once + nb, nh, (n + 1) % 2, safe)
                outs.append(second(h, n % 2, b, current))
                if h == HEADS - 1:
                    third(j * at_once + b, b, outs)
                    outs = []
            return carry

        lax.fori_loop(0, blocks // at_once, step, 0)

    @pl.when(bound <= SAFE_LOG2**2)
    def _():
        run(2, False)

    @pl.when(jnp.logical_not(bound <= SAFE_LOG2**2))
    def _():
        run(1, True)


def attend(tokens, cot, pool_sums, w_query, w_key, w_value, w_out, gain, bias):
    blocks, queries, features = tokens.shape
    keys = pool_sums.shape[0]
    flops = 2 * blocks * queries * features * (6 * keys + 6 * features)
    vmem = pl.BlockSpec(memory_space=pltpu.VMEM)
    return pl.pallas_call(
        attend_kernel,
        name="attend",
        out_shape=(
            jax.ShapeDtypeStruct((2 * keys + 2 * features, features), F32),
            jax.ShapeDtypeStruct((blocks, queries, features), BF16),
        ),
        in_specs=[vmem] * 9,
        out_specs=(vmem, vmem),
        scratch_shapes=[
            pltpu.VMEM((blocks, queries, features), BF16),
            pltpu.VMEM((blocks, features, queries), BF16),
            pltpu.VMEM((blocks, queries, features), BF16),
            pltpu.VMEM((blocks, features, queries), BF16),
            pltpu.VMEM((HEADS, keys, features), BF16),
            pltpu.VMEM((HEADS, keys, features), BF16),
            pltpu.VMEM((features, keys), BF16),
            pltpu.VMEM((features, keys), BF16),
            pltpu.VMEM((2, keys, queries), F32),
            pltpu.VMEM((2, keys, queries), F32),
            pltpu.VMEM((2, keys, HEADS * queries), BF16),
            pltpu.VMEM((2, keys, HEADS * queries), BF16),
        ],
        cost_estimate=pl.CostEstimate(
            flops=flops,
            bytes_accessed=3 * tokens.size * 2,
            transcendentals=blocks * queries * keys * HEADS,
        ),
        compiler_params=pltpu.CompilerParams(vmem_limit_bytes=48 * 1024 * 1024),
    )(tokens, cot, pool_sums, w_query, w_key, w_value, w_out, gain, bias)


def split_dot(low, wide):
    turned = low.astype(F32).T.astype(BF16)
    high = wide.astype(BF16)
    rest = wide - high.astype(F32)
    middle = rest.astype(BF16)
    last = (rest - middle.astype(F32)).astype(BF16)
    return dot(turned, high) + dot(turned, middle) + dot(turned, last)


def finish_kernel(
    grad_scale, sums_ref, pool_ref, dq_ref, w_query_ref, w_key_ref, w_value_ref, gain_ref,
    bias_ref, d_tokens_ref, d_query_ref, d_out_ref, d_key_ref, d_value_ref, d_gain_ref,
    d_bias_ref, pooled_grad_ref, own,
):
    keys, features = pool_ref.shape
    step = pl.program_id(0)
    cells_y, cells_x = 4, 8
    cells = cells_y * cells_x

    @pl.when(step == 0)
    def _():
        standard, inv_std = normalise(pool_ref[...])
        gain = gain_ref[...]
        normed_low = (standard * gain + bias_ref[...]).astype(BF16)
        key_grads = sums_ref[pl.ds(0, keys), :]
        value_grads = sums_ref[pl.ds(keys, keys), :]
        d_key_ref[...] = split_dot(normed_low, key_grads) * grad_scale
        d_value_ref[...] = split_dot(normed_low, value_grads) * grad_scale
        d_normed = dot_nt(key_grads.astype(BF16), w_key_ref[...]) + dot_nt(
            value_grads.astype(BF16), w_value_ref[...]
        )
        d_gain_ref[...] = jnp.sum(d_normed * standard, axis=0, keepdims=True) * grad_scale
        d_bias_ref[...] = jnp.sum(d_normed, axis=0, keepdims=True) * grad_scale
        scaled = d_normed * gain
        d_pooled = inv_std * (
            scaled
            - jnp.mean(scaled, axis=1, keepdims=True)
            - standard * jnp.mean(scaled * standard, axis=1, keepdims=True)
        )
        pooled_grad_ref[...] = d_pooled * grad_scale
        own[...] = d_pooled * (1.0 / float(POOL**3))
        d_query_ref[...] = sums_ref[pl.ds(2 * keys, features), :].T * grad_scale
        d_out_ref[...] = sums_ref[pl.ds(2 * keys + features, features), :] * grad_scale

    rows = dq_ref.shape[0]
    plane_x = cells_x * POOL
    me = lax.axis_index("gz")
    offset = (me // (2 * POOL) * 2 + lax.rem(me, 2)) * cells
    cell_y = step * rows // (plane_x * POOL)
    mine = own[pl.ds(pl.multiple_of(offset + cell_y * cells_x, 8), cells_x), :]
    spread = jnp.concatenate(
        [jnp.broadcast_to(mine[x : x + 1, :], (POOL, features)) for x in range(cells_x)], axis=0
    )
    product = dot_nt(dq_ref[...], w_query_ref[...])
    summed = product.reshape(rows // plane_x, plane_x, features) + spread[None]
    d_tokens_ref[...] = summed.reshape(rows, features).astype(BF16)


def finish(sums, pool_sums, dq, w_query, w_key, w_value, gain, bias, grad_scale):
    keys, features = pool_sums.shape
    tokens = dq.shape[0]
    rows = 1024

    def whole(*shape):
        return pl.BlockSpec(shape, lambda i: (0,) * len(shape))

    square = whole(features, features)
    line = whole(1, features)
    tile = pl.BlockSpec((rows, features), lambda i: (i, 0))
    return pl.pallas_call(
        functools.partial(finish_kernel, grad_scale),
        name="finish",
        grid=(tokens // rows,),
        out_shape=(
            jax.ShapeDtypeStruct((tokens, features), BF16),
            *[jax.ShapeDtypeStruct((features, features), F32)] * 4,
            *[jax.ShapeDtypeStruct((1, features), F32)] * 2,
            jax.ShapeDtypeStruct((keys, features), F32),
        ),
        in_specs=[
            whole(*sums.shape), whole(keys, features), tile, square, square, square, line, line,
        ],
        out_specs=(tile, square, square, square, square, line, line, whole(keys, features)),
        scratch_shapes=[pltpu.VMEM((keys, features), F32)],
        compiler_params=pltpu.CompilerParams(vmem_limit_bytes=32 * 1024 * 1024),
    )(sums, pool_sums, dq, w_query, w_key, w_value, gain, bias)


def body(tokens, cotangent, w_query, w_key, w_value, w_out, ln_gain, ln_bias):
    devices = lax.axis_size("gz")
    _, rows_y, plane_x, features = tokens.shape
    cells_y, cells_x = rows_y // POOL, plane_x // POOL
    slab_rows = rows_y * plane_x
    part = jnp.sum(
        tokens.astype(F32).reshape(cells_y, POOL, cells_x, POOL, features), axis=(1, 3)
    ).reshape(cells_y * cells_x, features)
    pool_sums = exchange_pools(part)
    gain, bias = ln_gain.reshape(1, features), ln_bias.reshape(1, features)
    blocks = slab_rows // QUERIES
    sums, dq = attend(
        tokens.reshape(blocks, QUERIES, features),
        cotangent.reshape(blocks, QUERIES, features),
        pool_sums, w_query, w_key, w_value, w_out, gain, bias,
    )
    sums = sum_devices(sums)
    grad_scale = float(devices * slab_rows) ** (-0.5)
    d_tokens, d_query, d_out, d_key, d_value, d_gain, d_bias, pooled_grad = finish(
        sums, pool_sums, dq.reshape(slab_rows, features), w_query, w_key, w_value, gain, bias,
        grad_scale,
    )
    return (
        d_tokens.reshape(1, rows_y, plane_x, features),
        d_query,
        d_out,
        d_key,
        d_value,
        d_gain.reshape(features),
        d_bias.reshape(features),
        pooled_grad,
    )


def solution(mesh):
    in_specs = (P("gz", None, None, None), P("gz", None, None, None), P(), P(), P(), P(), P(), P())
    out_specs = (P("gz", None, None, None), P(), P(), P(), P(), P(), P(), P())
    return jax.shard_map(body, mesh=mesh, in_specs=in_specs, out_specs=out_specs, check_vma=False)
```

```python
import functools
import math

import jax
import jax.numpy as jnp
from jax import lax
from jax.experimental import pallas as pl
from jax.experimental.pallas import tpu as pltpu
from jax.sharding import PartitionSpec as P

HEADS = 4
POOL = 16
EPSILON = 1e-05
MESH = pl.DeviceIdType.MESH
F32 = jnp.float32
BF16 = jnp.bfloat16

Z = 8
PLANE = 16
QUERIES = 256
KEY_CHUNK = 128
SAFE_LOG2 = 60.0


def dot(a, b):
    return lax.dot_general(a, b, (((1,), (0,)), ((), ())), preferred_element_type=F32)


def dot_nt(a, b):
    return lax.dot_general(a, b, (((1,), (1,)), ((), ())), preferred_element_type=F32)


def greet(partners):
    barrier = pltpu.get_barrier_semaphore()
    for partner in partners:
        pl.semaphore_signal(barrier, inc=1, device_id=(partner,), device_id_type=MESH)
    return lambda: pl.semaphore_wait(barrier, len(partners))


def send(src, dst, send_sem, recv_sem, partner):
    copy = pltpu.make_async_remote_copy(
        src_ref=src,
        dst_ref=dst,
        send_sem=send_sem,
        recv_sem=recv_sem,
        device_id=(partner,),
        device_id_type=MESH,
    )
    copy.start()
    return copy


def pool_kernel(
    tokens_ref, out_ref, pieces, got, near, far, sum_send, sum_recv, near_send, near_recv,
    far_send, far_recv,
):
    cells_y, _, plane_x, features = tokens_ref.shape
    cells_x = plane_x // POOL
    me = lax.axis_index("gz")
    core, chip = lax.rem(me, 2), me // 2
    member, block = lax.rem(chip, 16), chip // 16
    group = block * 2 + core
    members = [lax.rem(member + t, 16) for t in range(1, 16)]
    near_ids = [(block * 16 + other) * 2 + core for other in members]
    far_ids = []
    for t in range(1, 16):
        other = lax.rem(group + t, 16)
        far_ids.append(((other // 2) * 16 + member) * 2 + lax.rem(other, 2))
    await_partners = greet(near_ids + far_ids)

    share = got.shape[1]
    for y in range(cells_y):
        rows = jnp.sum(tokens_ref[y].astype(F32), axis=0)
        cells = jnp.sum(rows.reshape(cells_x, POOL, features), axis=1)
        for x in range(cells_x // share):
            pieces[y * (cells_x // share) + x] = cells[x * share : (x + 1) * share, :]
    await_partners()
    copies = [
        send(pieces.at[members[t]], got.at[t], sum_send.at[t], sum_recv.at[t], near_ids[t])
        for t in range(15)
    ]
    total = pieces[member]
    for t in range(15):
        copies[t].wait()
        total = total + got[t]

    near[member] = total
    copies = [
        send(near.at[member], near.at[member], near_send.at[t], near_recv.at[t], near_ids[t])
        for t in range(15)
    ]
    for copy in copies:
        copy.wait()
    for m in range(16):
        far[group, pl.ds(m * share, share), :] = near[m]

    copies = [
        send(far.at[group], far.at[group], far_send.at[t], far_recv.at[t], far_ids[t])
        for t in range(15)
    ]
    for copy in copies:
        copy.wait()
    for g in range(16):
        out_ref[pl.ds(g * 32, 32), :] = far[g]


def exchange_pools(tokens):
    cells_y, _, plane_x, features = tokens.shape
    rows = cells_y * (plane_x // POOL)
    dma = pltpu.SemaphoreType.DMA
    return pl.pallas_call(
        pool_kernel,
        name="pool_exchange",
        out_shape=jax.ShapeDtypeStruct((16 * rows, features), F32),
        in_specs=[pl.BlockSpec(memory_space=pltpu.VMEM)],
        out_specs=pl.BlockSpec(memory_space=pltpu.VMEM),
        scratch_shapes=[
            pltpu.VMEM((16, rows // 16, features), F32),
            pltpu.VMEM((15, rows // 16, features), F32),
            pltpu.VMEM((16, rows // 16, features), F32),
            pltpu.VMEM((16, rows, features), F32),
            *[dma((15,))] * 6,
        ],
        compiler_params=pltpu.CompilerParams(
            collective_id=0, has_side_effects=True, vmem_limit_bytes=8 * 1024 * 1024
        ),
    )(tokens)


STREAMS = ((0, 24), (24, 16))


def sum_kernel(
    w_ref, out_ref, got_half, half, got, along, full, pair_send, pair_recv, sum_send, sum_recv,
    z_send, z_recv, all_send, all_recv, back_send, back_recv,
):
    me = lax.axis_index("gz")
    core, chip = lax.rem(me, 2), me // 2
    z, plane = lax.rem(chip, Z), chip // Z
    sibling = me + 1 - 2 * core
    plane_members = [lax.rem(plane + t, PLANE) for t in range(1, PLANE)]
    plane_ids = [(other * Z + z) * 2 + core for other in plane_members]
    z_ids = [(plane * Z + lax.rem(z + t, Z)) * 2 + core for t in range(1, Z)]
    greet([sibling] + plane_ids + z_ids)()

    own = core * PLANE + plane
    mine = pl.ds(core * PLANE, PLANE)
    theirs = pl.ds((1 - core) * PLANE, PLANE)
    streams = range(len(STREAMS))
    rows = [pl.ds(*stream) for stream in STREAMS]

    pairs = [
        send(
            w_ref.at[theirs, rows[s]], got_half.at[:, rows[s]], pair_send.at[s], pair_recv.at[s],
            sibling,
        )
        for s in streams
    ]
    shares = []
    for s in streams:
        pairs[s].wait()
        half[:, rows[s], :] = w_ref[mine, rows[s], :] + got_half[:, rows[s], :]
        shares.append(
            [
                send(
                    half.at[plane_members[t], rows[s]], got.at[t, rows[s]], sum_send.at[s, t],
                    sum_recv.at[s, t], plane_ids[t],
                )
                for t in range(PLANE - 1)
            ]
        )
    lines = []
    for s in streams:
        total = half[plane, rows[s], :]
        for t in range(PLANE - 1):
            shares[s][t].wait()
            total = total + got[t, rows[s], :]
        along[z, rows[s], :] = total
        lines.append(
            [
                send(
                    along.at[z, rows[s]], along.at[z, rows[s]], z_send.at[s, t], z_recv.at[s, t],
                    z_ids[t],
                )
                for t in range(Z - 1)
            ]
        )
    gathers = []
    for s in streams:
        for copy in lines[s]:
            copy.wait()
        total = along[0, rows[s], :]
        for k in range(1, Z):
            total = total + along[k, rows[s], :]
        full[own, rows[s], :] = total
        gathers.append(
            [
                send(
                    full.at[own, rows[s]], full.at[own, rows[s]], all_send.at[s, t],
                    all_recv.at[s, t], plane_ids[t],
                )
                for t in range(PLANE - 1)
            ]
        )
    backs = []
    for s in streams:
        for copy in gathers[s]:
            copy.wait()
        backs.append(
            send(
                full.at[mine, rows[s]], full.at[mine, rows[s]], back_send.at[s], back_recv.at[s],
                sibling,
            )
        )
    for copy in backs:
        copy.wait()
    out_ref[...] = full[...]


def sum_devices(w):
    rows, features = w.shape
    share = rows // 2 // PLANE
    count = len(STREAMS)
    dma = pltpu.SemaphoreType.DMA
    return pl.pallas_call(
        sum_kernel,
        name="sum_devices",
        out_shape=jax.ShapeDtypeStruct((2 * PLANE, share, features), F32),
        in_specs=[pl.BlockSpec(memory_space=pltpu.VMEM)],
        out_specs=pl.BlockSpec(memory_space=pltpu.VMEM),
        scratch_shapes=[
            pltpu.VMEM((PLANE, share, features), F32),
            pltpu.VMEM((PLANE, share, features), F32),
            pltpu.VMEM((PLANE - 1, share, features), F32),
            pltpu.VMEM((Z, share, features), F32),
            pltpu.VMEM((2 * PLANE, share, features), F32),
            dma((count,)),
            dma((count,)),
            dma((count, PLANE - 1)),
            dma((count, PLANE - 1)),
            dma((count, Z - 1)),
            dma((count, Z - 1)),
            dma((count, PLANE - 1)),
            dma((count, PLANE - 1)),
            dma((count,)),
            dma((count,)),
        ],
        compiler_params=pltpu.CompilerParams(
            collective_id=1, has_side_effects=True, vmem_limit_bytes=10 * 1024 * 1024
        ),
    )(w.reshape(2 * PLANE, share, features)).reshape(rows, features)


def normalise(pool_sums):
    pooled = pool_sums * (1.0 / float(POOL**3))
    mean = jnp.mean(pooled, axis=1, keepdims=True)
    centered = pooled - mean
    var = jnp.mean(centered * centered, axis=1, keepdims=True)
    inv_std = lax.rsqrt(var + EPSILON)
    return centered * inv_std, inv_std


def transposed(w):
    return w.astype(F32).T.astype(BF16)


def three_terms(low, factor, lane_group):
    wide = low.astype(F32) * factor
    high = wide.astype(BF16)
    rest = wide - high.astype(F32)
    middle = rest.astype(BF16)
    last = (rest - middle.astype(F32)).astype(BF16)
    zero = jnp.zeros_like(high)
    return jnp.where(
        lane_group == 0,
        high,
        jnp.where(lane_group == 1, middle, jnp.where(lane_group == 2, last, zero)),
    )


def attend_kernel(
    tokens_ref, cot_ref, pool_ref, w_query_ref, w_key_ref, w_value_ref, w_out_ref, gain_ref,
    bias_ref, sums_ref, dq_ref, q_rows, q_cols, d_rows, d_cols, key_terms, value_terms, key_cols,
    value_cols, exps, dps, probs, dscores, key_sums, value_sums,
):
    blocks, queries, features = tokens_ref.shape
    keys = pool_ref.shape[0]
    head_dim = features // HEADS
    scale = head_dim ** (-0.5)
    chunks = keys // KEY_CHUNK

    standard, _ = normalise(pool_ref[...])
    normed_low = (standard * gain_ref[...] + bias_ref[...]).astype(BF16)
    source = lax.broadcasted_iota(jnp.int32, (features, HEADS * features), 0)
    target = lax.broadcasted_iota(jnp.int32, (features, HEADS * features), 1)
    spread = jnp.where(
        source == (target // features) * head_dim + lax.rem(target, head_dim), 1.0, 0.0
    ).astype(BF16)
    lane = lax.broadcasted_iota(jnp.int32, (keys, features), 1)
    lane_group = lane // head_dim
    for w_ref, factor, terms, cols in (
        (w_key_ref, scale * math.log2(math.e), key_terms, key_cols),
        (w_value_ref, scale, value_terms, value_cols),
    ):
        w = w_ref[...]
        wide_w = dot(w, spread).astype(BF16)
        for h in range(HEADS):
            low = dot(normed_low, wide_w[:, h * features : (h + 1) * features]).astype(BF16)
            terms[h] = three_terms(low, factor, lane_group)
        cols[...] = dot_nt(transposed(w), normed_low).astype(BF16)
    key_wide = key_cols[...].astype(F32).reshape(HEADS, head_dim, keys)
    key_norm = jnp.max(jnp.sum(key_wide * key_wide, axis=1), axis=1, keepdims=True)

    w_query = w_query_ref[...]
    w_query_t = transposed(w_query)
    w_out = w_out_ref[...]
    w_out_t = transposed(w_out)

    def project(i, norm):
        rows, grads = tokens_ref[i], cot_ref[i]
        q_rows[i] = dot(rows, w_query).astype(BF16)
        d_rows[i] = dot(grads, w_out_t).astype(BF16)
        cols = dot_nt(w_query_t, rows).astype(BF16)
        q_cols[i] = cols
        d_cols[i] = dot_nt(w_out, grads).astype(BF16)
        wide = cols.astype(F32).reshape(HEADS, head_dim, queries)
        return jnp.maximum(norm, jnp.sum(wide * wide, axis=1))

    norm = lax.fori_loop(0, blocks, project, jnp.zeros((HEADS, queries), F32))
    bound = jnp.max(norm * key_norm) * (scale * math.log2(math.e)) ** 2

    sums_ref[...] = jnp.zeros_like(sums_ref)
    key_sums[...] = jnp.zeros_like(key_sums)
    value_sums[...] = jnp.zeros_like(value_sums)
    def fold(x):
        return jnp.sum(x.reshape(x.shape[0] // 8, 8, queries), axis=0)

    def first(i, h, slot, safe):
        query = q_cols[i, h * head_dim : (h + 1) * head_dim, :]
        grad = d_cols[i, h * head_dim : (h + 1) * head_dim, :]
        query = jnp.concatenate([query] * HEADS, axis=0)
        grad = jnp.concatenate([grad] * HEADS, axis=0)
        total = jnp.zeros((8, queries), F32)
        delta = jnp.zeros((8, queries), F32)
        scores = dot(key_terms[h], query)
        d_probs = dot(value_terms[h], grad)
        if safe:
            scores = scores - jnp.max(scores, axis=0, keepdims=True)
        for c in range(chunks):
            part = slice(c * KEY_CHUNK, (c + 1) * KEY_CHUNK)
            e = jnp.exp2(scores[part, :])
            dp = d_probs[part, :]
            exps[slot, part, :] = e
            dps[slot, part, :] = dp
            total = total + fold(e)
            delta = delta + fold(e * dp)
        return total, delta

    def second(h, slot, bank, sums):
        total, delta = (jnp.sum(x, axis=0, keepdims=True) for x in sums)
        inverse = 1.0 / total
        delta = delta * inverse
        for c in range(chunks):
            part = pl.ds(c * KEY_CHUNK, KEY_CHUNK)
            rows = pl.ds(h * keys + c * KEY_CHUNK, KEY_CHUNK)
            p = exps[slot, part, :] * inverse
            probs[bank, rows, :] = p.astype(BF16)
            dscores[bank, rows, :] = (p * (dps[slot, part, :] - delta)).astype(BF16)
        head = pl.ds(h * head_dim, head_dim)
        rows = pl.ds(h * keys, keys)
        attn = dot(value_cols[head, :], probs[bank, rows, :])
        dq = dot(key_cols[head, :], dscores[bank, rows, :])
        return attn, dq

    def third(i, bank, outs):
        attn_low = jnp.concatenate([o[0] for o in outs], axis=0).astype(BF16)
        dq_low = jnp.concatenate([o[1] for o in outs], axis=0).astype(BF16)
        sums_ref[pl.ds(2 * keys, features), :] += dot(dq_low, tokens_ref[i])
        sums_ref[pl.ds(2 * keys + features, features), :] += dot(attn_low, cot_ref[i])
        dq_ref[i] = dq_low.astype(F32).T.astype(BF16)
        key_sums[...] += dot(dscores[bank], q_rows[i])
        value_sums[...] += dot(probs[bank], d_rows[i])

    def run(at_once, safe):
        def step(j, carry):
            units = [(b, h) for b in range(at_once) for h in range(HEADS)]
            pending = first(j * at_once, 0, 0, safe)
            outs = []
            for n, (b, h) in enumerate(units):
                current = pending
                if n + 1 < len(units):
                    nb, nh = units[n + 1]
                    pending = first(j * at_once + nb, nh, (n + 1) % 2, safe)
                outs.append(second(h, n % 2, b, current))
                if h == HEADS - 1:
                    third(j * at_once + b, b, outs)
                    outs = []
            return carry

        lax.fori_loop(0, blocks // at_once, step, 0)

    @pl.when(bound <= SAFE_LOG2**2)
    def _():
        run(2, False)

    @pl.when(jnp.logical_not(bound <= SAFE_LOG2**2))
    def _():
        run(1, True)

    for start, wide in ((0, key_sums), (keys, value_sums)):
        total = wide[pl.ds(0, keys), :]
        for h in range(1, HEADS):
            total = jnp.where(lane_group == h, wide[pl.ds(h * keys, keys), :], total)
        sums_ref[pl.ds(start, keys), :] = total


def attend(tokens, cot, pool_sums, w_query, w_key, w_value, w_out, gain, bias):
    blocks, queries, features = tokens.shape
    keys = pool_sums.shape[0]
    flops = 2 * blocks * queries * features * (6 * keys + 6 * features)
    vmem = pl.BlockSpec(memory_space=pltpu.VMEM)
    return pl.pallas_call(
        attend_kernel,
        name="attend",
        out_shape=(
            jax.ShapeDtypeStruct((2 * keys + 2 * features, features), F32),
            jax.ShapeDtypeStruct((blocks, queries, features), BF16),
        ),
        in_specs=[vmem] * 9,
        out_specs=(vmem, vmem),
        scratch_shapes=[
            pltpu.VMEM((blocks, queries, features), BF16),
            pltpu.VMEM((blocks, features, queries), BF16),
            pltpu.VMEM((blocks, queries, features), BF16),
            pltpu.VMEM((blocks, features, queries), BF16),
            pltpu.VMEM((HEADS, keys, features), BF16),
            pltpu.VMEM((HEADS, keys, features), BF16),
            pltpu.VMEM((features, keys), BF16),
            pltpu.VMEM((features, keys), BF16),
            pltpu.VMEM((2, keys, queries), F32),
            pltpu.VMEM((2, keys, queries), F32),
            pltpu.VMEM((2, HEADS * keys, queries), BF16),
            pltpu.VMEM((2, HEADS * keys, queries), BF16),
            pltpu.VMEM((HEADS * keys, features), F32),
            pltpu.VMEM((HEADS * keys, features), F32),
        ],
        cost_estimate=pl.CostEstimate(
            flops=flops,
            bytes_accessed=3 * tokens.size * 2,
            transcendentals=blocks * queries * keys * HEADS,
        ),
        compiler_params=pltpu.CompilerParams(vmem_limit_bytes=32 * 1024 * 1024),
    )(tokens, cot, pool_sums, w_query, w_key, w_value, w_out, gain, bias)


def split_dot(low, wide):
    turned = low.astype(F32).T.astype(BF16)
    high = wide.astype(BF16)
    rest = wide - high.astype(F32)
    middle = rest.astype(BF16)
    last = (rest - middle.astype(F32)).astype(BF16)
    return dot(turned, high) + dot(turned, middle) + dot(turned, last)


def finish_kernel(
    grad_scale, sums_ref, pool_ref, dq_ref, w_query_ref, w_key_ref, w_value_ref, gain_ref,
    bias_ref, d_tokens_ref, d_query_ref, d_out_ref, d_key_ref, d_value_ref, d_gain_ref,
    d_bias_ref, pooled_grad_ref, own,
):
    keys, features = pool_ref.shape
    step = pl.program_id(0)
    cells_y, cells_x = 4, 8
    cells = cells_y * cells_x

    @pl.when(step == 0)
    def _():
        standard, inv_std = normalise(pool_ref[...])
        gain = gain_ref[...]
        normed_low = (standard * gain + bias_ref[...]).astype(BF16)
        key_grads = sums_ref[pl.ds(0, keys), :]
        value_grads = sums_ref[pl.ds(keys, keys), :]
        both = split_dot(normed_low, jnp.concatenate([key_grads, value_grads], 1)) * grad_scale
        d_key_ref[...] = both[:, :features]
        d_value_ref[...] = both[:, features:]
        d_normed = dot_nt(key_grads.astype(BF16), w_key_ref[...]) + dot_nt(
            value_grads.astype(BF16), w_value_ref[...]
        )
        d_gain_ref[...] = jnp.sum(d_normed * standard, axis=0, keepdims=True) * grad_scale
        d_bias_ref[...] = jnp.sum(d_normed, axis=0, keepdims=True) * grad_scale
        scaled = d_normed * gain
        d_pooled = inv_std * (
            scaled
            - jnp.mean(scaled, axis=1, keepdims=True)
            - standard * jnp.mean(scaled * standard, axis=1, keepdims=True)
        )
        pooled_grad_ref[...] = d_pooled * grad_scale
        own[...] = d_pooled * (1.0 / float(POOL**3))
        d_query_ref[...] = sums_ref[pl.ds(2 * keys, features), :].T * grad_scale
        d_out_ref[...] = sums_ref[pl.ds(2 * keys + features, features), :] * grad_scale

    rows = dq_ref.shape[0]
    plane_x = cells_x * POOL
    me = lax.axis_index("gz")
    offset = (me // (2 * POOL) * 2 + lax.rem(me, 2)) * cells
    cell_y = step * rows // (plane_x * POOL)
    mine = own[pl.ds(pl.multiple_of(offset + cell_y * cells_x, 8), cells_x), :]
    spread = jnp.concatenate(
        [jnp.broadcast_to(mine[x : x + 1, :], (POOL, features)) for x in range(cells_x)], axis=0
    )
    product = dot_nt(dq_ref[...], w_query_ref[...])
    summed = product.reshape(rows // plane_x, plane_x, features) + spread[None]
    d_tokens_ref[...] = summed.reshape(rows, features).astype(BF16)


def finish(sums, pool_sums, dq, w_query, w_key, w_value, gain, bias, grad_scale):
    keys, features = pool_sums.shape
    tokens = dq.shape[0]
    rows = 1024

    def whole(*shape):
        return pl.BlockSpec(shape, lambda i: (0,) * len(shape))

    square = whole(features, features)
    line = whole(1, features)
    tile = pl.BlockSpec((rows, features), lambda i: (i, 0))
    return pl.pallas_call(
        functools.partial(finish_kernel, grad_scale),
        name="finish",
        grid=(tokens // rows,),
        out_shape=(
            jax.ShapeDtypeStruct((tokens, features), BF16),
            *[jax.ShapeDtypeStruct((features, features), F32)] * 4,
            *[jax.ShapeDtypeStruct((1, features), F32)] * 2,
            jax.ShapeDtypeStruct((keys, features), F32),
        ),
        in_specs=[
            whole(*sums.shape), whole(keys, features), tile, square, square, square, line, line,
        ],
        out_specs=(tile, square, square, square, square, line, line, whole(keys, features)),
        scratch_shapes=[pltpu.VMEM((keys, features), F32)],
        compiler_params=pltpu.CompilerParams(vmem_limit_bytes=16 * 1024 * 1024),
    )(sums, pool_sums, dq, w_query, w_key, w_value, gain, bias)


def body(tokens, cotangent, w_query, w_key, w_value, w_out, ln_gain, ln_bias):
    devices = lax.axis_size("gz")
    _, rows_y, plane_x, features = tokens.shape
    cells_y = rows_y // POOL
    slab_rows = rows_y * plane_x
    pool_sums = exchange_pools(tokens.reshape(cells_y, POOL, plane_x, features))
    gain, bias = ln_gain.reshape(1, features), ln_bias.reshape(1, features)
    blocks = slab_rows // QUERIES
    sums, dq = attend(
        tokens.reshape(blocks, QUERIES, features),
        cotangent.reshape(blocks, QUERIES, features),
        pool_sums, w_query, w_key, w_value, w_out, gain, bias,
    )
    sums = sum_devices(sums)
    grad_scale = float(devices * slab_rows) ** (-0.5)
    d_tokens, d_query, d_out, d_key, d_value, d_gain, d_bias, pooled_grad = finish(
        sums, pool_sums, dq.reshape(slab_rows, features), w_query, w_key, w_value, gain, bias,
        grad_scale,
    )
    return (
        d_tokens.reshape(1, rows_y, plane_x, features),
        d_query,
        d_out,
        d_key,
        d_value,
        d_gain.reshape(features),
        d_bias.reshape(features),
        pooled_grad,
    )


def solution(mesh):
    in_specs = (P("gz", None, None, None), P("gz", None, None, None), P(), P(), P(), P(), P(), P())
    out_specs = (P("gz", None, None, None), P(), P(), P(), P(), P(), P(), P())
    return jax.shard_map(body, mesh=mesh, in_specs=in_specs, out_specs=out_specs, check_vma=False)
```

```python
import functools
import math

import jax
import jax.numpy as jnp
from jax import lax
from jax.experimental import pallas as pl
from jax.experimental.pallas import tpu as pltpu
from jax.sharding import PartitionSpec as P

HEADS = 4
POOL = 16
EPSILON = 1e-05
MESH = pl.DeviceIdType.MESH
F32 = jnp.float32
BF16 = jnp.bfloat16

Z = 8
PLANE = 16
QUERIES = 512
KEY_CHUNK = 128
SAFE_LOG2 = 60.0


def dot(a, b):
    return lax.dot_general(a, b, (((1,), (0,)), ((), ())), preferred_element_type=F32)


def dot_nt(a, b):
    return lax.dot_general(a, b, (((1,), (1,)), ((), ())), preferred_element_type=F32)


def greet(partners):
    barrier = pltpu.get_barrier_semaphore()
    for partner in partners:
        pl.semaphore_signal(barrier, inc=1, device_id=(partner,), device_id_type=MESH)
    return lambda: pl.semaphore_wait(barrier, len(partners))


def send(src, dst, send_sem, recv_sem, partner):
    copy = pltpu.make_async_remote_copy(
        src_ref=src,
        dst_ref=dst,
        send_sem=send_sem,
        recv_sem=recv_sem,
        device_id=(partner,),
        device_id_type=MESH,
    )
    copy.start()
    return copy


LOADS = 4


def pool_kernel(
    tokens_hbm, cot_hbm, w_query_ref, w_out_ref, out_ref, tokens_ref, cot_ref, q_rows, q_cols,
    d_rows, d_cols, norm_ref, pieces, got, near, far, load_sem, sum_send, sum_recv, near_send,
    near_recv, far_send, far_recv,
):
    blocks, queries, features = tokens_ref.shape
    head_dim = features // HEADS
    plane_x = queries // 4
    cells_x = plane_x // POOL
    part = blocks // LOADS
    loads = [
        pltpu.make_async_copy(
            source.at[pl.ds(n * part, part)], target.at[pl.ds(n * part, part)],
            load_sem.at[k, n],
        )
        for k, (source, target) in enumerate(((tokens_hbm, tokens_ref), (cot_hbm, cot_ref)))
        for n in range(LOADS)
    ]
    for load in loads:
        load.start()

    me = lax.axis_index("gz")
    core, chip = lax.rem(me, 2), me // 2
    member, block = lax.rem(chip, 16), chip // 16
    group = block * 2 + core
    members = [lax.rem(member + t, 16) for t in range(1, 16)]
    near_ids = [(block * 16 + other) * 2 + core for other in members]
    far_ids = []
    for t in range(1, 16):
        other = lax.rem(group + t, 16)
        far_ids.append(((other // 2) * 16 + member) * 2 + lax.rem(other, 2))
    await_partners = greet(near_ids + far_ids)

    share = got.shape[1]
    for y in range(LOADS):
        loads[y].wait()
        rows = jnp.zeros((plane_x, features), F32)
        for b in range(y * part, (y + 1) * part):
            wide = tokens_ref[b].astype(F32)
            for k in range(queries // plane_x):
                rows = rows + wide[k * plane_x : (k + 1) * plane_x, :]
        cells = jnp.sum(rows.reshape(cells_x, POOL, features), axis=1)
        for x in range(cells_x // share):
            pieces[y * (cells_x // share) + x] = cells[x * share : (x + 1) * share, :]
    await_partners()
    copies = [
        send(pieces.at[members[t]], got.at[t], sum_send.at[t], sum_recv.at[t], near_ids[t])
        for t in range(15)
    ]

    w_query = w_query_ref[...]
    w_query_t = transposed(w_query)
    w_out = w_out_ref[...]
    w_out_t = transposed(w_out)

    def project_tokens(i, norm):
        rows = tokens_ref[i]
        q_rows[i] = dot(rows, w_query).astype(BF16)
        cols = dot_nt(w_query_t, rows).astype(BF16)
        q_cols[i] = cols
        wide = cols.astype(F32).reshape(HEADS, head_dim, queries)
        return jnp.maximum(norm, jnp.sum(wide * wide, axis=1))

    def project_grads(i, carry):
        grads = cot_ref[i]
        d_rows[i] = dot(grads, w_out_t).astype(BF16)
        d_cols[i] = dot_nt(w_out, grads).astype(BF16)
        return carry

    norm_ref[...] = lax.fori_loop(
        0, blocks, project_tokens, jnp.zeros((HEADS, queries), F32)
    )

    total = pieces[member]
    for t in range(15):
        copies[t].wait()
        total = total + got[t]
    near[member] = total
    copies = [
        send(near.at[member], near.at[member], near_send.at[t], near_recv.at[t], near_ids[t])
        for t in range(15)
    ]
    for load in loads[LOADS:]:
        load.wait()
    lax.fori_loop(0, blocks // 2, project_grads, 0)
    for copy in copies:
        copy.wait()
    for m in range(16):
        far[group, pl.ds(m * share, share), :] = near[m]

    copies = [
        send(far.at[group], far.at[group], far_send.at[t], far_recv.at[t], far_ids[t])
        for t in range(15)
    ]
    lax.fori_loop(blocks // 2, blocks, project_grads, 0)
    for copy in copies:
        copy.wait()
    for g in range(16):
        out_ref[pl.ds(g * 32, 32), :] = far[g]


def exchange_pools(tokens, cot, w_query, w_out):
    blocks, queries, features = tokens.shape
    rows = 32
    dma = pltpu.SemaphoreType.DMA
    vmem = pl.BlockSpec(memory_space=pltpu.VMEM)
    hbm = pl.BlockSpec(memory_space=pl.ANY)
    by_rows = jax.ShapeDtypeStruct((blocks, queries, features), BF16)
    by_cols = jax.ShapeDtypeStruct((blocks, features, queries), BF16)
    return pl.pallas_call(
        pool_kernel,
        name="pool_exchange",
        out_shape=(
            jax.ShapeDtypeStruct((16 * rows, features), F32),
            by_rows, by_rows, by_rows, by_cols, by_rows, by_cols,
            jax.ShapeDtypeStruct((HEADS, queries), F32),
        ),
        in_specs=[hbm, hbm, vmem, vmem],
        out_specs=(vmem,) * 8,
        scratch_shapes=[
            pltpu.VMEM((16, rows // 16, features), F32),
            pltpu.VMEM((15, rows // 16, features), F32),
            pltpu.VMEM((16, rows // 16, features), F32),
            pltpu.VMEM((16, rows, features), F32),
            dma((2, LOADS)),
            *[dma((15,))] * 6,
        ],
        compiler_params=pltpu.CompilerParams(
            collective_id=0, has_side_effects=True, vmem_limit_bytes=40 * 1024 * 1024
        ),
    )(tokens, cot, w_query, w_out)


STREAMS = ((0, 24), (24, 16))


def sum_kernel(
    w_ref, out_ref, got_half, half, got, along, full, pair_send, pair_recv, sum_send, sum_recv,
    z_send, z_recv, all_send, all_recv, back_send, back_recv,
):
    me = lax.axis_index("gz")
    core, chip = lax.rem(me, 2), me // 2
    z, plane = lax.rem(chip, Z), chip // Z
    sibling = me + 1 - 2 * core
    plane_members = [lax.rem(plane + t, PLANE) for t in range(1, PLANE)]
    plane_ids = [(other * Z + z) * 2 + core for other in plane_members]
    z_ids = [(plane * Z + lax.rem(z + t, Z)) * 2 + core for t in range(1, Z)]
    greet([sibling] + plane_ids + z_ids)()

    own = core * PLANE + plane
    mine = pl.ds(core * PLANE, PLANE)
    theirs = pl.ds((1 - core) * PLANE, PLANE)
    streams = range(len(STREAMS))
    rows = [pl.ds(*stream) for stream in STREAMS]

    pairs = [
        send(
            w_ref.at[theirs, rows[s]], got_half.at[:, rows[s]], pair_send.at[s], pair_recv.at[s],
            sibling,
        )
        for s in streams
    ]
    shares = []
    for s in streams:
        pairs[s].wait()
        half[:, rows[s], :] = w_ref[mine, rows[s], :] + got_half[:, rows[s], :]
        shares.append(
            [
                send(
                    half.at[plane_members[t], rows[s]], got.at[t, rows[s]], sum_send.at[s, t],
                    sum_recv.at[s, t], plane_ids[t],
                )
                for t in range(PLANE - 1)
            ]
        )
    lines = []
    for s in streams:
        total = half[plane, rows[s], :]
        for t in range(PLANE - 1):
            shares[s][t].wait()
            total = total + got[t, rows[s], :]
        along[z, rows[s], :] = total
        lines.append(
            [
                send(
                    along.at[z, rows[s]], along.at[z, rows[s]], z_send.at[s, t], z_recv.at[s, t],
                    z_ids[t],
                )
                for t in range(Z - 1)
            ]
        )
    gathers = []
    for s in streams:
        for copy in lines[s]:
            copy.wait()
        total = along[0, rows[s], :]
        for k in range(1, Z):
            total = total + along[k, rows[s], :]
        full[own, rows[s], :] = total
        gathers.append(
            [
                send(
                    full.at[own, rows[s]], full.at[own, rows[s]], all_send.at[s, t],
                    all_recv.at[s, t], plane_ids[t],
                )
                for t in range(PLANE - 1)
            ]
        )
    backs = []
    for s in streams:
        for copy in gathers[s]:
            copy.wait()
        backs.append(
            send(
                full.at[mine, rows[s]], full.at[mine, rows[s]], back_send.at[s], back_recv.at[s],
                sibling,
            )
        )
    for copy in backs:
        copy.wait()
    out_ref[...] = full[...]


def sum_devices(w):
    rows, features = w.shape
    share = rows // 2 // PLANE
    count = len(STREAMS)
    dma = pltpu.SemaphoreType.DMA
    return pl.pallas_call(
        sum_kernel,
        name="sum_devices",
        out_shape=jax.ShapeDtypeStruct((2 * PLANE, share, features), F32),
        in_specs=[pl.BlockSpec(memory_space=pltpu.VMEM)],
        out_specs=pl.BlockSpec(memory_space=pltpu.VMEM),
        scratch_shapes=[
            pltpu.VMEM((PLANE, share, features), F32),
            pltpu.VMEM((PLANE, share, features), F32),
            pltpu.VMEM((PLANE - 1, share, features), F32),
            pltpu.VMEM((Z, share, features), F32),
            pltpu.VMEM((2 * PLANE, share, features), F32),
            dma((count,)),
            dma((count,)),
            dma((count, PLANE - 1)),
            dma((count, PLANE - 1)),
            dma((count, Z - 1)),
            dma((count, Z - 1)),
            dma((count, PLANE - 1)),
            dma((count, PLANE - 1)),
            dma((count,)),
            dma((count,)),
        ],
        compiler_params=pltpu.CompilerParams(
            collective_id=1, has_side_effects=True, vmem_limit_bytes=10 * 1024 * 1024
        ),
    )(w.reshape(2 * PLANE, share, features)).reshape(rows, features)


def normalise(pool_sums):
    pooled = pool_sums * (1.0 / float(POOL**3))
    mean = jnp.mean(pooled, axis=1, keepdims=True)
    centered = pooled - mean
    var = jnp.mean(centered * centered, axis=1, keepdims=True)
    inv_std = lax.rsqrt(var + EPSILON)
    return centered * inv_std, inv_std


def transposed(w):
    return w.astype(F32).T.astype(BF16)


def three_terms(low, factor, lane_group):
    wide = low.astype(F32) * factor
    high = wide.astype(BF16)
    rest = wide - high.astype(F32)
    middle = rest.astype(BF16)
    last = (rest - middle.astype(F32)).astype(BF16)
    zero = jnp.zeros_like(high)
    return jnp.where(
        lane_group == 0,
        high,
        jnp.where(lane_group == 1, middle, jnp.where(lane_group == 2, last, zero)),
    )


def attend_kernel(
    tokens_ref, cot_ref, pool_ref, q_rows, q_cols, d_rows, d_cols, norm_ref, w_key_ref,
    w_value_ref, gain_ref, bias_ref, sums_ref, dq_ref, key_terms, value_terms, key_cols,
    value_cols, exps, dps, probs, dscores, key_sums, value_sums,
):
    blocks, queries, features = tokens_ref.shape
    keys = pool_ref.shape[0]
    head_dim = features // HEADS
    scale = head_dim ** (-0.5)
    chunks = keys // KEY_CHUNK

    standard, _ = normalise(pool_ref[...])
    normed_low = (standard * gain_ref[...] + bias_ref[...]).astype(BF16)
    source = lax.broadcasted_iota(jnp.int32, (features, HEADS * features), 0)
    target = lax.broadcasted_iota(jnp.int32, (features, HEADS * features), 1)
    spread = jnp.where(
        source == (target // features) * head_dim + lax.rem(target, head_dim), 1.0, 0.0
    ).astype(BF16)
    lane = lax.broadcasted_iota(jnp.int32, (keys, features), 1)
    lane_group = lane // head_dim
    for w_ref, factor, terms, cols in (
        (w_key_ref, scale * math.log2(math.e), key_terms, key_cols),
        (w_value_ref, scale, value_terms, value_cols),
    ):
        w = w_ref[...]
        wide_w = dot(w, spread).astype(BF16)
        for h in range(HEADS):
            low = dot(normed_low, wide_w[:, h * features : (h + 1) * features]).astype(BF16)
            terms[h] = three_terms(low, factor, lane_group)
        cols[...] = dot_nt(transposed(w), normed_low).astype(BF16)
    key_wide = key_cols[...].astype(F32).reshape(HEADS, head_dim, keys)
    key_norm = jnp.max(jnp.sum(key_wide * key_wide, axis=1), axis=1, keepdims=True)

    bound = jnp.max(norm_ref[...] * key_norm) * (scale * math.log2(math.e)) ** 2

    sums_ref[...] = jnp.zeros_like(sums_ref)
    key_sums[...] = jnp.zeros_like(key_sums)
    value_sums[...] = jnp.zeros_like(value_sums)
    def fold(x):
        return jnp.sum(x.reshape(x.shape[0] // 8, 8, queries), axis=0)

    def first(i, h, slot, safe):
        query = q_cols[i, h * head_dim : (h + 1) * head_dim, :]
        grad = d_cols[i, h * head_dim : (h + 1) * head_dim, :]
        query = jnp.concatenate([query] * HEADS, axis=0)
        grad = jnp.concatenate([grad] * HEADS, axis=0)
        total = jnp.zeros((8, queries), F32)
        delta = jnp.zeros((8, queries), F32)
        scores = dot(key_terms[h], query)
        d_probs = dot(value_terms[h], grad)
        if safe:
            scores = scores - jnp.max(scores, axis=0, keepdims=True)
        for c in range(chunks):
            part = slice(c * KEY_CHUNK, (c + 1) * KEY_CHUNK)
            e = jnp.exp2(scores[part, :])
            dp = d_probs[part, :]
            exps[slot, part, :] = e
            dps[slot, part, :] = dp
            total = total + fold(e)
            delta = delta + fold(e * dp)
        return total, delta

    def second(h, slot, sums):
        total, delta = (jnp.sum(x, axis=0, keepdims=True) for x in sums)
        inverse = 1.0 / total
        delta = delta * inverse
        for c in range(chunks):
            part = pl.ds(c * KEY_CHUNK, KEY_CHUNK)
            rows = pl.ds(h * keys + c * KEY_CHUNK, KEY_CHUNK)
            p = exps[slot, part, :] * inverse
            probs[rows, :] = p.astype(BF16)
            dscores[rows, :] = (p * (dps[slot, part, :] - delta)).astype(BF16)
        head = pl.ds(h * head_dim, head_dim)
        rows = pl.ds(h * keys, keys)
        attn = dot(value_cols[head, :], probs[rows, :])
        dq = dot(key_cols[head, :], dscores[rows, :])
        return attn, dq

    def over_keys(i, outs):
        attn_low = jnp.concatenate([o[0] for o in outs], axis=0).astype(BF16)
        dq_low = jnp.concatenate([o[1] for o in outs], axis=0).astype(BF16)
        sums_ref[pl.ds(2 * keys, features), :] += dot(dq_low, tokens_ref[i])
        sums_ref[pl.ds(2 * keys + features, features), :] += dot(attn_low, cot_ref[i])
        dq_ref[i] = dq_low.astype(F32).T.astype(BF16)

    def over_queries(i):
        key_sums[...] += dot(dscores[...], q_rows[i])
        value_sums[...] += dot(probs[...], d_rows[i])

    def run(safe):
        def step(i, carry):
            pending = [first(i, 0, 0, safe), first(i, 1, 1, safe)]
            over_queries(jnp.maximum(i - 1, 0))
            outs = []
            for h in range(HEADS):
                outs.append(second(h, h % 2, pending[h]))
                if h + 2 < HEADS:
                    pending.append(first(i, h + 2, h % 2, safe))
            over_keys(i, outs)
            return carry

        lax.fori_loop(0, blocks, step, 0)

    probs[...] = jnp.zeros_like(probs)
    dscores[...] = jnp.zeros_like(dscores)

    @pl.when(bound <= SAFE_LOG2**2)
    def _():
        run(False)

    @pl.when(jnp.logical_not(bound <= SAFE_LOG2**2))
    def _():
        run(True)

    over_queries(blocks - 1)

    for start, wide in ((0, key_sums), (keys, value_sums)):
        total = wide[pl.ds(0, keys), :]
        for h in range(1, HEADS):
            total = jnp.where(lane_group == h, wide[pl.ds(h * keys, keys), :], total)
        sums_ref[pl.ds(start, keys), :] = total


def attend(tokens, cot, pool_sums, q_rows, q_cols, d_rows, d_cols, norm, w_key, w_value, gain, bias):
    blocks, queries, features = tokens.shape
    keys = pool_sums.shape[0]
    flops = 2 * blocks * queries * features * (6 * keys + 2 * features)
    vmem = pl.BlockSpec(memory_space=pltpu.VMEM)
    return pl.pallas_call(
        attend_kernel,
        name="attend",
        out_shape=(
            jax.ShapeDtypeStruct((2 * keys + 2 * features, features), F32),
            jax.ShapeDtypeStruct((blocks, queries, features), BF16),
        ),
        in_specs=[vmem] * 12,
        out_specs=(vmem, vmem),
        scratch_shapes=[
            pltpu.VMEM((HEADS, keys, features), BF16),
            pltpu.VMEM((HEADS, keys, features), BF16),
            pltpu.VMEM((features, keys), BF16),
            pltpu.VMEM((features, keys), BF16),
            pltpu.VMEM((2, keys, queries), F32),
            pltpu.VMEM((2, keys, queries), F32),
            pltpu.VMEM((HEADS * keys, queries), BF16),
            pltpu.VMEM((HEADS * keys, queries), BF16),
            pltpu.VMEM((HEADS * keys, features), F32),
            pltpu.VMEM((HEADS * keys, features), F32),
        ],
        cost_estimate=pl.CostEstimate(
            flops=flops,
            bytes_accessed=3 * tokens.size * 2,
            transcendentals=blocks * queries * keys * HEADS,
        ),
        compiler_params=pltpu.CompilerParams(vmem_limit_bytes=28 * 1024 * 1024),
    )(tokens, cot, pool_sums, q_rows, q_cols, d_rows, d_cols, norm, w_key, w_value, gain, bias)


def split_dot(low, wide):
    turned = low.astype(F32).T.astype(BF16)
    high = wide.astype(BF16)
    rest = wide - high.astype(F32)
    middle = rest.astype(BF16)
    last = (rest - middle.astype(F32)).astype(BF16)
    return dot(turned, high) + dot(turned, middle) + dot(turned, last)


def finish_kernel(
    grad_scale, sums_ref, pool_ref, dq_ref, w_query_ref, w_key_ref, w_value_ref, gain_ref,
    bias_ref, d_tokens_ref, d_query_ref, d_out_ref, d_key_ref, d_value_ref, d_gain_ref,
    d_bias_ref, pooled_grad_ref, own,
):
    keys, features = pool_ref.shape
    step = pl.program_id(0)
    cells_y, cells_x = 4, 8
    cells = cells_y * cells_x

    @pl.when(step == 0)
    def _():
        standard, inv_std = normalise(pool_ref[...])
        gain = gain_ref[...]
        normed_low = (standard * gain + bias_ref[...]).astype(BF16)
        key_grads = sums_ref[pl.ds(0, keys), :]
        value_grads = sums_ref[pl.ds(keys, keys), :]
        both = split_dot(normed_low, jnp.concatenate([key_grads, value_grads], 1)) * grad_scale
        d_key_ref[...] = both[:, :features]
        d_value_ref[...] = both[:, features:]
        d_normed = dot_nt(key_grads.astype(BF16), w_key_ref[...]) + dot_nt(
            value_grads.astype(BF16), w_value_ref[...]
        )
        d_gain_ref[...] = jnp.sum(d_normed * standard, axis=0, keepdims=True) * grad_scale
        d_bias_ref[...] = jnp.sum(d_normed, axis=0, keepdims=True) * grad_scale
        scaled = d_normed * gain
        d_pooled = inv_std * (
            scaled
            - jnp.mean(scaled, axis=1, keepdims=True)
            - standard * jnp.mean(scaled * standard, axis=1, keepdims=True)
        )
        pooled_grad_ref[...] = d_pooled * grad_scale
        own[...] = d_pooled * (1.0 / float(POOL**3))
        d_query_ref[...] = sums_ref[pl.ds(2 * keys, features), :].T * grad_scale
        d_out_ref[...] = sums_ref[pl.ds(2 * keys + features, features), :] * grad_scale

    rows = dq_ref.shape[0]
    plane_x = cells_x * POOL
    me = lax.axis_index("gz")
    offset = (me // (2 * POOL) * 2 + lax.rem(me, 2)) * cells
    cell_y = step * rows // (plane_x * POOL)
    mine = own[pl.ds(pl.multiple_of(offset + cell_y * cells_x, 8), cells_x), :]
    spread = jnp.concatenate(
        [jnp.broadcast_to(mine[x : x + 1, :], (POOL, features)) for x in range(cells_x)], axis=0
    )
    product = dot_nt(dq_ref[...], w_query_ref[...])
    summed = product.reshape(rows // plane_x, plane_x, features) + spread[None]
    d_tokens_ref[...] = summed.reshape(rows, features).astype(BF16)


def finish(sums, pool_sums, dq, w_query, w_key, w_value, gain, bias, grad_scale):
    keys, features = pool_sums.shape
    tokens = dq.shape[0]
    rows = 2048

    def whole(*shape):
        return pl.BlockSpec(shape, lambda i: (0,) * len(shape))

    square = whole(features, features)
    line = whole(1, features)
    tile = pl.BlockSpec((rows, features), lambda i: (i, 0))
    return pl.pallas_call(
        functools.partial(finish_kernel, grad_scale),
        name="finish",
        grid=(tokens // rows,),
        out_shape=(
            jax.ShapeDtypeStruct((tokens, features), BF16),
            *[jax.ShapeDtypeStruct((features, features), F32)] * 4,
            *[jax.ShapeDtypeStruct((1, features), F32)] * 2,
            jax.ShapeDtypeStruct((keys, features), F32),
        ),
        in_specs=[
            whole(*sums.shape), whole(keys, features), tile, square, square, square, line, line,
        ],
        out_specs=(tile, square, square, square, square, line, line, whole(keys, features)),
        scratch_shapes=[pltpu.VMEM((keys, features), F32)],
        compiler_params=pltpu.CompilerParams(vmem_limit_bytes=16 * 1024 * 1024),
    )(sums, pool_sums, dq, w_query, w_key, w_value, gain, bias)


def body(tokens, cotangent, w_query, w_key, w_value, w_out, ln_gain, ln_bias):
    devices = lax.axis_size("gz")
    _, rows_y, plane_x, features = tokens.shape
    slab_rows = rows_y * plane_x
    gain, bias = ln_gain.reshape(1, features), ln_bias.reshape(1, features)
    blocks = slab_rows // QUERIES
    pool_sums, token_rows, cot_rows, q_rows, q_cols, d_rows, d_cols, norm = exchange_pools(
        tokens.reshape(blocks, QUERIES, features),
        cotangent.reshape(blocks, QUERIES, features),
        w_query, w_out,
    )
    sums, dq = attend(
        token_rows, cot_rows, pool_sums, q_rows, q_cols, d_rows, d_cols, norm, w_key, w_value,
        gain, bias,
    )
    sums = sum_devices(sums)
    grad_scale = float(devices * slab_rows) ** (-0.5)
    d_tokens, d_query, d_out, d_key, d_value, d_gain, d_bias, pooled_grad = finish(
        sums, pool_sums, dq.reshape(slab_rows, features), w_query, w_key, w_value, gain, bias,
        grad_scale,
    )
    return (
        d_tokens.reshape(1, rows_y, plane_x, features),
        d_query,
        d_out,
        d_key,
        d_value,
        d_gain.reshape(features),
        d_bias.reshape(features),
        pooled_grad,
    )


def solution(mesh):
    in_specs = (P("gz", None, None, None), P("gz", None, None, None), P(), P(), P(), P(), P(), P())
    out_specs = (P("gz", None, None, None), P(), P(), P(), P(), P(), P(), P())
    return jax.shard_map(body, mesh=mesh, in_specs=in_specs, out_specs=out_specs, check_vma=False)
```

```python
import functools

import jax
import jax.numpy as jnp
from jax import lax
from jax.experimental import pallas as pl
from jax.experimental.pallas import tpu as pltpu
from jax.sharding import PartitionSpec as P

HEADS = 4
POOL = 16
EPSILON = 1e-05
MESH = pl.DeviceIdType.MESH
F32 = jnp.float32
BF16 = jnp.bfloat16

Z = 8
PLANE = 16
QUERIES = 512
KEY_CHUNK = 256
SAFE = 40.0


def dot(a, b):
    return lax.dot_general(a, b, (((1,), (0,)), ((), ())), preferred_element_type=F32)


def dot_nt(a, b):
    return lax.dot_general(a, b, (((1,), (1,)), ((), ())), preferred_element_type=F32)


def greet(partners):
    barrier = pltpu.get_barrier_semaphore()
    for partner in partners:
        pl.semaphore_signal(barrier, inc=1, device_id=(partner,), device_id_type=MESH)
    return lambda: pl.semaphore_wait(barrier, len(partners))


def send(src, dst, send_sem, recv_sem, partner):
    copy = pltpu.make_async_remote_copy(
        src_ref=src,
        dst_ref=dst,
        send_sem=send_sem,
        recv_sem=recv_sem,
        device_id=(partner,),
        device_id_type=MESH,
    )
    copy.start()
    return copy


LOADS = 4


def pool_kernel(
    tokens_hbm, cot_hbm, weights_ref, out_ref, tokens_ref, cot_ref, q_rows, q_cols,
    d_rows, d_cols, norm_ref, pieces, got, near, far, load_sem, sum_send, sum_recv, near_send,
    near_recv, far_send, far_recv,
):
    blocks, queries, features = tokens_ref.shape
    head_dim = features // HEADS
    plane_x = queries // 4
    cells_x = plane_x // POOL
    part = blocks // LOADS
    loads = [
        pltpu.make_async_copy(
            source.at[pl.ds(n * part, part)], target.at[pl.ds(n * part, part)],
            load_sem.at[k, n],
        )
        for k, (source, target) in enumerate(((tokens_hbm, tokens_ref), (cot_hbm, cot_ref)))
        for n in range(LOADS)
    ]
    for load in loads:
        load.start()

    me = lax.axis_index("gz")
    core, chip = lax.rem(me, 2), me // 2
    member, block = lax.rem(chip, 16), chip // 16
    group = block * 2 + core
    members = [lax.rem(member + t, 16) for t in range(1, 16)]
    near_ids = [(block * 16 + other) * 2 + core for other in members]
    far_ids = []
    for t in range(1, 16):
        other = lax.rem(group + t, 16)
        far_ids.append(((other // 2) * 16 + member) * 2 + lax.rem(other, 2))
    await_partners = greet(near_ids + far_ids)

    share = got.shape[1]
    for y in range(LOADS):
        loads[y].wait()
        rows = jnp.zeros((plane_x, features), F32)
        for b in range(y * part, (y + 1) * part):
            wide = tokens_ref[b].astype(F32)
            for k in range(queries // plane_x):
                rows = rows + wide[k * plane_x : (k + 1) * plane_x, :]
        cells = jnp.sum(rows.reshape(cells_x, POOL, features), axis=1)
        for x in range(cells_x // share):
            pieces[y * (cells_x // share) + x] = cells[x * share : (x + 1) * share, :]
    await_partners()
    copies = [
        send(pieces.at[members[t]], got.at[t], sum_send.at[t], sum_recv.at[t], near_ids[t])
        for t in range(15)
    ]

    w_query = weights_ref[:features, :]
    w_query_t = transposed(w_query)
    w_out = weights_ref[features:, :]
    w_out_t = transposed(w_out)

    def project_tokens(i, norm):
        rows = tokens_ref[i]
        q_rows[i] = dot(rows, w_query).astype(BF16)
        cols = dot_nt(w_query_t, rows).astype(BF16)
        q_cols[i] = cols
        wide = cols.astype(F32).reshape(HEADS, head_dim, queries)
        return jnp.maximum(norm, jnp.sum(wide * wide, axis=1))

    def project_grads(i, carry):
        grads = cot_ref[i]
        d_rows[i] = dot(grads, w_out_t).astype(BF16)
        d_cols[i] = dot_nt(w_out, grads).astype(BF16)
        return carry

    norm_ref[...] = lax.fori_loop(
        0, blocks, project_tokens, jnp.zeros((HEADS, queries), F32)
    )

    total = pieces[member]
    for t in range(15):
        copies[t].wait()
        total = total + got[t]
    near[member] = total
    copies = [
        send(near.at[member], near.at[member], near_send.at[t], near_recv.at[t], near_ids[t])
        for t in range(15)
    ]
    for load in loads[LOADS:]:
        load.wait()
    lax.fori_loop(0, blocks // 2, project_grads, 0)
    for copy in copies:
        copy.wait()
    for m in range(16):
        far[group, pl.ds(m * share, share), :] = near[m]

    copies = [
        send(far.at[group], far.at[group], far_send.at[t], far_recv.at[t], far_ids[t])
        for t in range(15)
    ]
    lax.fori_loop(blocks // 2, blocks, project_grads, 0)
    for copy in copies:
        copy.wait()
    for g in range(16):
        out_ref[pl.ds(g * 32, 32), :] = far[g]


def exchange_pools(tokens, cot, weights):
    blocks, queries, features = tokens.shape
    rows = 32
    dma = pltpu.SemaphoreType.DMA
    vmem = pl.BlockSpec(memory_space=pltpu.VMEM)
    hbm = pl.BlockSpec(memory_space=pl.ANY)
    by_rows = jax.ShapeDtypeStruct((blocks, queries, features), BF16)
    by_cols = jax.ShapeDtypeStruct((blocks, features, queries), BF16)
    return pl.pallas_call(
        pool_kernel,
        name="pool_exchange",
        out_shape=(
            jax.ShapeDtypeStruct((16 * rows, features), F32),
            by_rows, by_rows, by_rows, by_cols, by_rows, by_cols,
            jax.ShapeDtypeStruct((HEADS, queries), F32),
        ),
        in_specs=[hbm, hbm, vmem],
        out_specs=(vmem,) * 8,
        scratch_shapes=[
            pltpu.VMEM((16, rows // 16, features), F32),
            pltpu.VMEM((15, rows // 16, features), F32),
            pltpu.VMEM((16, rows // 16, features), F32),
            pltpu.VMEM((16, rows, features), F32),
            dma((2, LOADS)),
            *[dma((15,))] * 6,
        ],
        compiler_params=pltpu.CompilerParams(
            collective_id=0, has_side_effects=True, vmem_limit_bytes=40 * 1024 * 1024
        ),
    )(tokens, cot, weights)


STREAMS = ((0, 24), (24, 16))


def sum_kernel(
    w_ref, out_ref, got_half, half, got, along, full, pair_send, pair_recv, sum_send, sum_recv,
    z_send, z_recv, all_send, all_recv, back_send, back_recv,
):
    me = lax.axis_index("gz")
    core, chip = lax.rem(me, 2), me // 2
    z, plane = lax.rem(chip, Z), chip // Z
    sibling = me + 1 - 2 * core
    plane_members = [lax.rem(plane + t, PLANE) for t in range(1, PLANE)]
    plane_ids = [(other * Z + z) * 2 + core for other in plane_members]
    z_ids = [(plane * Z + lax.rem(z + t, Z)) * 2 + core for t in range(1, Z)]
    greet([sibling] + plane_ids + z_ids)()

    own = core * PLANE + plane
    mine = pl.ds(core * PLANE, PLANE)
    theirs = pl.ds((1 - core) * PLANE, PLANE)
    streams = range(len(STREAMS))
    rows = [pl.ds(*stream) for stream in STREAMS]

    pairs = [
        send(
            w_ref.at[theirs, rows[s]], got_half.at[:, rows[s]], pair_send.at[s], pair_recv.at[s],
            sibling,
        )
        for s in streams
    ]
    shares = []
    for s in streams:
        pairs[s].wait()
        half[:, rows[s], :] = w_ref[mine, rows[s], :] + got_half[:, rows[s], :]
        shares.append(
            [
                send(
                    half.at[plane_members[t], rows[s]], got.at[t, rows[s]], sum_send.at[s, t],
                    sum_recv.at[s, t], plane_ids[t],
                )
                for t in range(PLANE - 1)
            ]
        )
    lines = []
    for s in streams:
        total = half[plane, rows[s], :]
        for t in range(PLANE - 1):
            shares[s][t].wait()
            total = total + got[t, rows[s], :]
        along[z, rows[s], :] = total
        lines.append(
            [
                send(
                    along.at[z, rows[s]], along.at[z, rows[s]], z_send.at[s, t], z_recv.at[s, t],
                    z_ids[t],
                )
                for t in range(Z - 1)
            ]
        )
    gathers = []
    for s in streams:
        for copy in lines[s]:
            copy.wait()
        total = along[0, rows[s], :]
        for k in range(1, Z):
            total = total + along[k, rows[s], :]
        full[own, rows[s], :] = total
        gathers.append(
            [
                send(
                    full.at[own, rows[s]], full.at[own, rows[s]], all_send.at[s, t],
                    all_recv.at[s, t], plane_ids[t],
                )
                for t in range(PLANE - 1)
            ]
        )
    backs = []
    for s in streams:
        for copy in gathers[s]:
            copy.wait()
        backs.append(
            send(
                full.at[mine, rows[s]], full.at[mine, rows[s]], back_send.at[s], back_recv.at[s],
                sibling,
            )
        )
    for copy in backs:
        copy.wait()
    out_ref[...] = full[...]


def sum_devices(w):
    rows, features = w.shape
    share = rows // 2 // PLANE
    count = len(STREAMS)
    dma = pltpu.SemaphoreType.DMA
    return pl.pallas_call(
        sum_kernel,
        name="sum_devices",
        out_shape=jax.ShapeDtypeStruct((2 * PLANE, share, features), F32),
        in_specs=[pl.BlockSpec(memory_space=pltpu.VMEM)],
        out_specs=pl.BlockSpec(memory_space=pltpu.VMEM),
        scratch_shapes=[
            pltpu.VMEM((PLANE, share, features), F32),
            pltpu.VMEM((PLANE, share, features), F32),
            pltpu.VMEM((PLANE - 1, share, features), F32),
            pltpu.VMEM((Z, share, features), F32),
            pltpu.VMEM((2 * PLANE, share, features), F32),
            dma((count,)),
            dma((count,)),
            dma((count, PLANE - 1)),
            dma((count, PLANE - 1)),
            dma((count, Z - 1)),
            dma((count, Z - 1)),
            dma((count, PLANE - 1)),
            dma((count, PLANE - 1)),
            dma((count,)),
            dma((count,)),
        ],
        compiler_params=pltpu.CompilerParams(
            collective_id=1, has_side_effects=True, vmem_limit_bytes=10 * 1024 * 1024
        ),
    )(w.reshape(2 * PLANE, share, features)).reshape(rows, features)


def normalise(pool_sums):
    pooled = pool_sums * (1.0 / float(POOL**3))
    mean = jnp.mean(pooled, axis=1, keepdims=True)
    centered = pooled - mean
    var = jnp.mean(centered * centered, axis=1, keepdims=True)
    inv_std = lax.rsqrt(var + EPSILON)
    return centered * inv_std, inv_std


def transposed(w):
    return w.astype(F32).T.astype(BF16)


def three_terms(low, factor, lane_group):
    wide = low.astype(F32) * factor
    high = wide.astype(BF16)
    rest = wide - high.astype(F32)
    middle = rest.astype(BF16)
    last = (rest - middle.astype(F32)).astype(BF16)
    zero = jnp.zeros_like(high)
    return jnp.where(
        lane_group == 0,
        high,
        jnp.where(lane_group == 1, middle, jnp.where(lane_group == 2, last, zero)),
    )


def attend_kernel(
    tokens_ref, cot_ref, pool_ref, q_rows, q_cols, d_rows, d_cols, norm_ref, w_key_ref,
    w_value_ref, gain_ref, bias_ref, sums_ref, dq_ref, key_terms, value_terms, key_cols,
    value_cols, exps, dps, probs, dscores, key_sums, value_sums, attn_low, dq_low,
):
    blocks, queries, features = tokens_ref.shape
    keys = pool_ref.shape[0]
    head_dim = features // HEADS
    scale = head_dim ** (-0.5)
    chunks = keys // KEY_CHUNK

    standard, _ = normalise(pool_ref[...])
    normed_low = (standard * gain_ref[...] + bias_ref[...]).astype(BF16)
    source = lax.broadcasted_iota(jnp.int32, (features, HEADS * features), 0)
    target = lax.broadcasted_iota(jnp.int32, (features, HEADS * features), 1)
    spread = jnp.where(
        source == (target // features) * head_dim + lax.rem(target, head_dim), 1.0, 0.0
    ).astype(BF16)
    lane = lax.broadcasted_iota(jnp.int32, (keys, features), 1)
    lane_group = lane // head_dim
    for w_ref, factor, terms, cols in (
        (w_key_ref, scale, key_terms, key_cols),
        (w_value_ref, scale, value_terms, value_cols),
    ):
        w = w_ref[...]
        wide_w = dot(w, spread).astype(BF16)
        for h in range(HEADS):
            low = dot(normed_low, wide_w[:, h * features : (h + 1) * features]).astype(BF16)
            terms[h] = three_terms(low, factor, lane_group)
        cols[...] = dot_nt(transposed(w), normed_low).astype(BF16)
    key_wide = key_cols[...].astype(F32).reshape(HEADS, head_dim, keys)
    key_norm = jnp.max(jnp.sum(key_wide * key_wide, axis=1), axis=1, keepdims=True)

    bound = jnp.max(norm_ref[...] * key_norm) * scale**2

    sums_ref[...] = jnp.zeros_like(sums_ref)
    key_sums[...] = jnp.zeros_like(key_sums)
    value_sums[...] = jnp.zeros_like(value_sums)
    def fold(x):
        return jnp.sum(x.reshape(x.shape[0] // 8, 8, queries), axis=0)

    def operands(i, h):
        head = pl.ds(h * head_dim, head_dim)
        query, grad = q_cols[i, head, :], d_cols[i, head, :]
        return jnp.concatenate([query] * HEADS, axis=0), jnp.concatenate([grad] * HEADS, axis=0)

    def head_over_keys(h):
        head = pl.ds(h * head_dim, head_dim)
        rows = pl.ds(h * keys, keys)
        attn_low[head, :] = dot(value_cols[head, :], probs[rows, :]).astype(BF16)
        dq_low[head, :] = dot(key_cols[head, :], dscores[rows, :]).astype(BF16)

    def block_over_keys(i):
        dq = dq_low[...]
        sums_ref[pl.ds(2 * keys, features), :] += dot(dq, tokens_ref[i])
        sums_ref[pl.ds(2 * keys + features, features), :] += dot(attn_low[...], cot_ref[i])
        dq_ref[i] = dq.astype(F32).T.astype(BF16)

    def keys_over_queries(i, h):
        rows = pl.ds(h * keys, keys)
        key_sums[rows, :] += dot(dscores[rows, :], q_rows[i])

    def values_over_queries(i, h):
        rows = pl.ds(h * keys, keys)
        value_sums[rows, :] += dot(probs[rows, :], d_rows[i])

    def stage(i, h, sums, safe, only_first=False):
        following = (h + 1) % HEADS
        at = i if following else jnp.minimum(i + 1, blocks - 1)
        summed = jnp.maximum(i - 1, 0) if following else i
        query, grad = operands(at, following)
        slot, later = h % 2, following % 2
        if not only_first:
            total, delta = (jnp.sum(x, axis=0, keepdims=True) for x in sums)
            inverse = 1.0 / total
            delta = delta * inverse
        next_total = jnp.zeros((8, queries), F32)
        next_delta = jnp.zeros((8, queries), F32)
        if safe:
            scores = dot(key_terms[following], query)
            scores = scores - jnp.max(scores, axis=0, keepdims=True)
        for c in range(chunks):
            part = slice(c * KEY_CHUNK, (c + 1) * KEY_CHUNK)
            s = scores[part, :] if safe else dot(key_terms[following, part, :], query)
            dp = dot(value_terms[following, part, :], grad)
            if not only_first:
                if c == 0:
                    head_over_keys((h - 1) % HEADS)
                    keys_over_queries(summed, following)
                if c == chunks - 1:
                    values_over_queries(summed, following)
                    if h == 0:
                        block_over_keys(summed)
                rows = pl.ds(h * keys + c * KEY_CHUNK, KEY_CHUNK)
                p = exps[slot, part, :] * inverse
                probs[rows, :] = p.astype(BF16)
                dscores[rows, :] = (p * (dps[slot, part, :] - delta)).astype(BF16)
            e = jnp.exp(s)
            exps[later, part, :] = e
            dps[later, part, :] = dp
            next_total = next_total + fold(e)
            next_delta = next_delta + fold(e * dp)
        return next_total, next_delta

    def run(safe):
        def step(i, sums):
            for h in range(HEADS):
                sums = stage(i, h, sums, safe)
            return sums

        sums = stage(jnp.int32(-1), HEADS - 1, None, safe, only_first=True)
        lax.fori_loop(0, blocks, step, sums)

    for ref in (probs, dscores, attn_low, dq_low):
        ref[...] = jnp.zeros_like(ref)

    @pl.when(bound <= SAFE**2)
    def _():
        run(False)

    @pl.when(jnp.logical_not(bound <= SAFE**2))
    def _():
        run(True)

    head_over_keys(HEADS - 1)
    block_over_keys(blocks - 1)
    for h in range(1, HEADS):
        keys_over_queries(blocks - 1, h)
        values_over_queries(blocks - 1, h)

    for start, wide in ((0, key_sums), (keys, value_sums)):
        total = wide[pl.ds(0, keys), :]
        for h in range(1, HEADS):
            total = jnp.where(lane_group == h, wide[pl.ds(h * keys, keys), :], total)
        sums_ref[pl.ds(start, keys), :] = total


def attend(tokens, cot, pool_sums, q_rows, q_cols, d_rows, d_cols, norm, w_key, w_value, gain, bias):
    blocks, queries, features = tokens.shape
    keys = pool_sums.shape[0]
    flops = 2 * blocks * queries * features * (6 * keys + 2 * features)
    vmem = pl.BlockSpec(memory_space=pltpu.VMEM)
    return pl.pallas_call(
        attend_kernel,
        name="attend",
        out_shape=(
            jax.ShapeDtypeStruct((2 * keys + 2 * features, features), F32),
            jax.ShapeDtypeStruct((blocks, queries, features), BF16),
        ),
        in_specs=[vmem] * 12,
        out_specs=(vmem, vmem),
        scratch_shapes=[
            pltpu.VMEM((HEADS, keys, features), BF16),
            pltpu.VMEM((HEADS, keys, features), BF16),
            pltpu.VMEM((features, keys), BF16),
            pltpu.VMEM((features, keys), BF16),
            pltpu.VMEM((2, keys, queries), F32),
            pltpu.VMEM((2, keys, queries), F32),
            pltpu.VMEM((HEADS * keys, queries), BF16),
            pltpu.VMEM((HEADS * keys, queries), BF16),
            pltpu.VMEM((HEADS * keys, features), F32),
            pltpu.VMEM((HEADS * keys, features), F32),
            pltpu.VMEM((features, queries), BF16),
            pltpu.VMEM((features, queries), BF16),
        ],
        cost_estimate=pl.CostEstimate(
            flops=flops,
            bytes_accessed=3 * tokens.size * 2,
            transcendentals=blocks * queries * keys * HEADS,
        ),
        compiler_params=pltpu.CompilerParams(vmem_limit_bytes=28 * 1024 * 1024),
    )(tokens, cot, pool_sums, q_rows, q_cols, d_rows, d_cols, norm, w_key, w_value, gain, bias)


def split_dot(low, wide):
    turned = low.astype(F32).T.astype(BF16)
    high = wide.astype(BF16)
    rest = wide - high.astype(F32)
    middle = rest.astype(BF16)
    last = (rest - middle.astype(F32)).astype(BF16)
    return dot(turned, high) + dot(turned, middle) + dot(turned, last)


def finish_kernel(
    grad_scale, sums_ref, pool_ref, dq_ref, w_query_ref, w_key_ref, w_value_ref, gain_ref,
    bias_ref, d_tokens_ref, d_query_ref, d_out_ref, d_key_ref, d_value_ref, d_gain_ref,
    d_bias_ref, pooled_grad_ref, own,
):
    keys, features = pool_ref.shape
    step = pl.program_id(0)
    cells_y, cells_x = 4, 8
    cells = cells_y * cells_x

    @pl.when(step == 0)
    def _():
        standard, inv_std = normalise(pool_ref[...])
        gain = gain_ref[...]
        normed_low = (standard * gain + bias_ref[...]).astype(BF16)
        key_grads = sums_ref[pl.ds(0, keys), :]
        value_grads = sums_ref[pl.ds(keys, keys), :]
        both = split_dot(normed_low, jnp.concatenate([key_grads, value_grads], 1)) * grad_scale
        d_key_ref[...] = both[:, :features]
        d_value_ref[...] = both[:, features:]
        d_normed = dot_nt(key_grads.astype(BF16), w_key_ref[...]) + dot_nt(
            value_grads.astype(BF16), w_value_ref[...]
        )
        d_gain_ref[...] = jnp.sum(d_normed * standard, axis=0, keepdims=True) * grad_scale
        d_bias_ref[...] = jnp.sum(d_normed, axis=0, keepdims=True) * grad_scale
        scaled = d_normed * gain
        d_pooled = inv_std * (
            scaled
            - jnp.mean(scaled, axis=1, keepdims=True)
            - standard * jnp.mean(scaled * standard, axis=1, keepdims=True)
        )
        pooled_grad_ref[...] = d_pooled * grad_scale
        own[...] = d_pooled * (1.0 / float(POOL**3))
        d_query_ref[...] = sums_ref[pl.ds(2 * keys, features), :].T * grad_scale
        d_out_ref[...] = sums_ref[pl.ds(2 * keys + features, features), :] * grad_scale

    rows = dq_ref.shape[0]
    plane_x = cells_x * POOL
    me = lax.axis_index("gz")
    offset = (me // (2 * POOL) * 2 + lax.rem(me, 2)) * cells
    cell_y = step * rows // (plane_x * POOL)
    mine = own[pl.ds(pl.multiple_of(offset + cell_y * cells_x, 8), cells_x), :]
    spread = jnp.concatenate(
        [jnp.broadcast_to(mine[x : x + 1, :], (POOL, features)) for x in range(cells_x)], axis=0
    )
    product = dot_nt(dq_ref[...], w_query_ref[...])
    summed = product.reshape(rows // plane_x, plane_x, features) + spread[None]
    d_tokens_ref[...] = summed.reshape(rows, features).astype(BF16)


def finish(sums, pool_sums, dq, w_query, w_key, w_value, gain, bias, grad_scale):
    keys, features = pool_sums.shape
    tokens = dq.shape[0]
    rows = 2048

    def whole(*shape):
        return pl.BlockSpec(shape, lambda i: (0,) * len(shape))

    square = whole(features, features)
    line = whole(1, features)
    tile = pl.BlockSpec((rows, features), lambda i: (i, 0))
    return pl.pallas_call(
        functools.partial(finish_kernel, grad_scale),
        name="finish",
        grid=(tokens // rows,),
        out_shape=(
            jax.ShapeDtypeStruct((tokens, features), BF16),
            *[jax.ShapeDtypeStruct((features, features), F32)] * 4,
            *[jax.ShapeDtypeStruct((1, features), F32)] * 2,
            jax.ShapeDtypeStruct((keys, features), F32),
        ),
        in_specs=[
            whole(*sums.shape), whole(keys, features), tile, square, square, square, line, line,
        ],
        out_specs=(tile, square, square, square, square, line, line, whole(keys, features)),
        scratch_shapes=[pltpu.VMEM((keys, features), F32)],
        compiler_params=pltpu.CompilerParams(vmem_limit_bytes=16 * 1024 * 1024),
    )(sums, pool_sums, dq, w_query, w_key, w_value, gain, bias)


def body(tokens, cotangent, w_query, w_key, w_value, w_out, ln_gain, ln_bias):
    devices = lax.axis_size("gz")
    _, rows_y, plane_x, features = tokens.shape
    slab_rows = rows_y * plane_x
    gain, bias = ln_gain.reshape(1, features), ln_bias.reshape(1, features)
    blocks = slab_rows // QUERIES
    pool_sums, token_rows, cot_rows, q_rows, q_cols, d_rows, d_cols, norm = exchange_pools(
        tokens.reshape(blocks, QUERIES, features),
        cotangent.reshape(blocks, QUERIES, features),
        jnp.concatenate([w_query, w_out], axis=0),
    )
    sums, dq = attend(
        token_rows, cot_rows, pool_sums, q_rows, q_cols, d_rows, d_cols, norm, w_key, w_value,
        gain, bias,
    )
    sums = sum_devices(sums)
    grad_scale = float(devices * slab_rows) ** (-0.5)
    d_tokens, d_query, d_out, d_key, d_value, d_gain, d_bias, pooled_grad = finish(
        sums, pool_sums, dq.reshape(slab_rows, features), w_query, w_key, w_value, gain, bias,
        grad_scale,
    )
    return (
        d_tokens.reshape(1, rows_y, plane_x, features),
        d_query,
        d_out,
        d_key,
        d_value,
        d_gain.reshape(features),
        d_bias.reshape(features),
        pooled_grad,
    )


def solution(mesh):
    in_specs = (P("gz", None, None, None), P("gz", None, None, None), P(), P(), P(), P(), P(), P())
    out_specs = (P("gz", None, None, None), P(), P(), P(), P(), P(), P(), P())
    return jax.shard_map(body, mesh=mesh, in_specs=in_specs, out_specs=out_specs, check_vma=False)
```

```python
import functools

import jax
import jax.numpy as jnp
from jax import lax
from jax.experimental import pallas as pl
from jax.experimental.pallas import tpu as pltpu
from jax.sharding import PartitionSpec as P

HEADS = 4
POOL = 16
EPSILON = 1e-05
MESH = pl.DeviceIdType.MESH
F32 = jnp.float32
BF16 = jnp.bfloat16

Z = 8
PLANE = 16
QUERIES = 512
KEY_CHUNK = 256
SAFE = 40.0


def dot(a, b):
    return lax.dot_general(a, b, (((1,), (0,)), ((), ())), preferred_element_type=F32)


def dot_nt(a, b):
    return lax.dot_general(a, b, (((1,), (1,)), ((), ())), preferred_element_type=F32)


def greet(partners):
    barrier = pltpu.get_barrier_semaphore()
    for partner in partners:
        pl.semaphore_signal(barrier, inc=1, device_id=(partner,), device_id_type=MESH)
    return lambda: pl.semaphore_wait(barrier, len(partners))


def send(src, dst, send_sem, recv_sem, partner):
    copy = pltpu.make_async_remote_copy(
        src_ref=src,
        dst_ref=dst,
        send_sem=send_sem,
        recv_sem=recv_sem,
        device_id=(partner,),
        device_id_type=MESH,
    )
    copy.start()
    return copy


LOADS = 4


def pool_kernel(
    tokens_hbm, cot_hbm, weights_ref, out_ref, tokens_ref, cot_ref, q_cols, d_cols, norm_ref, pieces, got, near, far, load_sem, sum_send, sum_recv, near_send,
    near_recv, far_send, far_recv,
):
    blocks, queries, features = tokens_ref.shape
    head_dim = features // HEADS
    plane_x = queries // 4
    cells_x = plane_x // POOL
    part = blocks // LOADS
    loads = [
        pltpu.make_async_copy(
            source.at[pl.ds(n * part, part)], target.at[pl.ds(n * part, part)],
            load_sem.at[k, n],
        )
        for k, (source, target) in enumerate(((tokens_hbm, tokens_ref), (cot_hbm, cot_ref)))
        for n in range(LOADS)
    ]
    for load in loads:
        load.start()

    me = lax.axis_index("gz")
    core, chip = lax.rem(me, 2), me // 2
    member, block = lax.rem(chip, 16), chip // 16
    group = block * 2 + core
    members = [lax.rem(member + t, 16) for t in range(1, 16)]
    near_ids = [(block * 16 + other) * 2 + core for other in members]
    far_ids = []
    for t in range(1, 16):
        other = lax.rem(group + t, 16)
        far_ids.append(((other // 2) * 16 + member) * 2 + lax.rem(other, 2))
    await_partners = greet(near_ids + far_ids)

    share = got.shape[1]
    for y in range(LOADS):
        loads[y].wait()
        rows = jnp.zeros((plane_x, features), F32)
        for b in range(y * part, (y + 1) * part):
            wide = tokens_ref[b].astype(F32)
            for k in range(queries // plane_x):
                rows = rows + wide[k * plane_x : (k + 1) * plane_x, :]
        cells = jnp.sum(rows.reshape(cells_x, POOL, features), axis=1)
        for x in range(cells_x // share):
            pieces[y * (cells_x // share) + x] = cells[x * share : (x + 1) * share, :]
    await_partners()
    copies = [
        send(pieces.at[members[t]], got.at[t], sum_send.at[t], sum_recv.at[t], near_ids[t])
        for t in range(15)
    ]

    w_query_t = transposed(weights_ref[:features, :])
    w_out = weights_ref[features:, :]

    def project_tokens(i, norm):
        cols = dot_nt(w_query_t, tokens_ref[i]).astype(BF16)
        q_cols[i] = cols
        wide = cols.astype(F32).reshape(HEADS, head_dim, queries)
        return jnp.maximum(norm, jnp.sum(wide * wide, axis=1))

    def project_grads(i, carry):
        d_cols[i] = dot_nt(w_out, cot_ref[i]).astype(BF16)
        return carry

    norm_ref[...] = lax.fori_loop(
        0, blocks, project_tokens, jnp.zeros((HEADS, queries), F32)
    )

    total = pieces[member]
    for t in range(15):
        copies[t].wait()
        total = total + got[t]
    near[member] = total
    copies = [
        send(near.at[member], near.at[member], near_send.at[t], near_recv.at[t], near_ids[t])
        for t in range(15)
    ]
    for load in loads[LOADS:]:
        load.wait()
    lax.fori_loop(0, blocks // 2, project_grads, 0)
    for copy in copies:
        copy.wait()
    for m in range(16):
        far[group, pl.ds(m * share, share), :] = near[m]

    copies = [
        send(far.at[group], far.at[group], far_send.at[t], far_recv.at[t], far_ids[t])
        for t in range(15)
    ]
    lax.fori_loop(blocks // 2, blocks, project_grads, 0)
    for copy in copies:
        copy.wait()
    for g in range(16):
        out_ref[pl.ds(g * 32, 32), :] = far[g]


def exchange_pools(tokens, cot, weights):
    blocks, queries, features = tokens.shape
    rows = 32
    dma = pltpu.SemaphoreType.DMA
    vmem = pl.BlockSpec(memory_space=pltpu.VMEM)
    hbm = pl.BlockSpec(memory_space=pl.ANY)
    by_rows = jax.ShapeDtypeStruct((blocks, queries, features), BF16)
    by_cols = jax.ShapeDtypeStruct((blocks, features, queries), BF16)
    return pl.pallas_call(
        pool_kernel,
        name="pool_exchange",
        out_shape=(
            jax.ShapeDtypeStruct((16 * rows, features), F32),
            by_rows, by_rows, by_cols, by_cols,
            jax.ShapeDtypeStruct((HEADS, queries), F32),
        ),
        in_specs=[hbm, hbm, vmem],
        out_specs=(vmem,) * 6,
        scratch_shapes=[
            pltpu.VMEM((16, rows // 16, features), F32),
            pltpu.VMEM((15, rows // 16, features), F32),
            pltpu.VMEM((16, rows // 16, features), F32),
            pltpu.VMEM((16, rows, features), F32),
            dma((2, LOADS)),
            *[dma((15,))] * 6,
        ],
        compiler_params=pltpu.CompilerParams(
            collective_id=0, has_side_effects=True, vmem_limit_bytes=44 * 1024 * 1024
        ),
    )(tokens, cot, weights)


STREAMS = ((0, 24), (24, 16))


def sum_kernel(
    w_ref, out_ref, got_half, half, got, along, full, pair_send, pair_recv, sum_send, sum_recv,
    z_send, z_recv, all_send, all_recv, back_send, back_recv,
):
    me = lax.axis_index("gz")
    core, chip = lax.rem(me, 2), me // 2
    z, plane = lax.rem(chip, Z), chip // Z
    sibling = me + 1 - 2 * core
    plane_members = [lax.rem(plane + t, PLANE) for t in range(1, PLANE)]
    plane_ids = [(other * Z + z) * 2 + core for other in plane_members]
    z_ids = [(plane * Z + lax.rem(z + t, Z)) * 2 + core for t in range(1, Z)]
    greet([sibling] + plane_ids + z_ids)()

    own = core * PLANE + plane
    mine = pl.ds(core * PLANE, PLANE)
    theirs = pl.ds((1 - core) * PLANE, PLANE)
    streams = range(len(STREAMS))
    rows = [pl.ds(*stream) for stream in STREAMS]

    pairs = [
        send(
            w_ref.at[theirs, rows[s]], got_half.at[:, rows[s]], pair_send.at[s], pair_recv.at[s],
            sibling,
        )
        for s in streams
    ]
    shares = []
    for s in streams:
        pairs[s].wait()
        half[:, rows[s], :] = w_ref[mine, rows[s], :] + got_half[:, rows[s], :]
        shares.append(
            [
                send(
                    half.at[plane_members[t], rows[s]], got.at[t, rows[s]], sum_send.at[s, t],
                    sum_recv.at[s, t], plane_ids[t],
                )
                for t in range(PLANE - 1)
            ]
        )
    lines = []
    for s in streams:
        total = half[plane, rows[s], :]
        for t in range(PLANE - 1):
            shares[s][t].wait()
            total = total + got[t, rows[s], :]
        along[z, rows[s], :] = total
        lines.append(
            [
                send(
                    along.at[z, rows[s]], along.at[z, rows[s]], z_send.at[s, t], z_recv.at[s, t],
                    z_ids[t],
                )
                for t in range(Z - 1)
            ]
        )
    gathers = []
    for s in streams:
        for copy in lines[s]:
            copy.wait()
        total = along[0, rows[s], :]
        for k in range(1, Z):
            total = total + along[k, rows[s], :]
        full[own, rows[s], :] = total
        gathers.append(
            [
                send(
                    full.at[own, rows[s]], full.at[own, rows[s]], all_send.at[s, t],
                    all_recv.at[s, t], plane_ids[t],
                )
                for t in range(PLANE - 1)
            ]
        )
    backs = []
    for s in streams:
        for copy in gathers[s]:
            copy.wait()
        backs.append(
            send(
                full.at[mine, rows[s]], full.at[mine, rows[s]], back_send.at[s], back_recv.at[s],
                sibling,
            )
        )
    for copy in backs:
        copy.wait()
    out_ref[...] = full[...]


def sum_devices(w):
    rows, features = w.shape
    share = rows // 2 // PLANE
    count = len(STREAMS)
    dma = pltpu.SemaphoreType.DMA
    return pl.pallas_call(
        sum_kernel,
        name="sum_devices",
        out_shape=jax.ShapeDtypeStruct((2 * PLANE, share, features), F32),
        in_specs=[pl.BlockSpec(memory_space=pltpu.VMEM)],
        out_specs=pl.BlockSpec(memory_space=pltpu.VMEM),
        scratch_shapes=[
            pltpu.VMEM((PLANE, share, features), F32),
            pltpu.VMEM((PLANE, share, features), F32),
            pltpu.VMEM((PLANE - 1, share, features), F32),
            pltpu.VMEM((Z, share, features), F32),
            pltpu.VMEM((2 * PLANE, share, features), F32),
            dma((count,)),
            dma((count,)),
            dma((count, PLANE - 1)),
            dma((count, PLANE - 1)),
            dma((count, Z - 1)),
            dma((count, Z - 1)),
            dma((count, PLANE - 1)),
            dma((count, PLANE - 1)),
            dma((count,)),
            dma((count,)),
        ],
        compiler_params=pltpu.CompilerParams(
            collective_id=1, has_side_effects=True, vmem_limit_bytes=10 * 1024 * 1024
        ),
    )(w.reshape(2 * PLANE, share, features)).reshape(rows, features)


def normalise(pool_sums):
    pooled = pool_sums * (1.0 / float(POOL**3))
    mean = jnp.mean(pooled, axis=1, keepdims=True)
    centered = pooled - mean
    var = jnp.mean(centered * centered, axis=1, keepdims=True)
    inv_std = lax.rsqrt(var + EPSILON)
    return centered * inv_std, inv_std


def transposed(w):
    return w.astype(F32).T.astype(BF16)


def three_terms(low, factor, lane_group):
    wide = low.astype(F32) * factor
    high = wide.astype(BF16)
    rest = wide - high.astype(F32)
    middle = rest.astype(BF16)
    last = (rest - middle.astype(F32)).astype(BF16)
    zero = jnp.zeros_like(high)
    return jnp.where(
        lane_group == 0,
        high,
        jnp.where(lane_group == 1, middle, jnp.where(lane_group == 2, last, zero)),
    )


def attend_kernel(
    tokens_ref, cot_ref, pool_ref, q_cols, d_cols, norm_ref, w_key_ref,
    w_value_ref, gain_ref, bias_ref, sums_ref, dq_ref, key_terms, value_terms, key_cols,
    value_cols, exps, dps, probs, dscores, key_sums, value_sums, attn_low, dq_low,
):
    blocks, queries, features = tokens_ref.shape
    keys = pool_ref.shape[0]
    head_dim = features // HEADS
    scale = head_dim ** (-0.5)
    chunks = keys // KEY_CHUNK

    standard, _ = normalise(pool_ref[...])
    normed_low = (standard * gain_ref[...] + bias_ref[...]).astype(BF16)
    source = lax.broadcasted_iota(jnp.int32, (features, HEADS * features), 0)
    target = lax.broadcasted_iota(jnp.int32, (features, HEADS * features), 1)
    spread = jnp.where(
        source == (target // features) * head_dim + lax.rem(target, head_dim), 1.0, 0.0
    ).astype(BF16)
    lane = lax.broadcasted_iota(jnp.int32, (keys, features), 1)
    lane_group = lane // head_dim
    for w_ref, factor, terms, cols in (
        (w_key_ref, scale, key_terms, key_cols),
        (w_value_ref, scale, value_terms, value_cols),
    ):
        w = w_ref[...]
        wide_w = dot(w, spread).astype(BF16)
        for h in range(HEADS):
            low = dot(normed_low, wide_w[:, h * features : (h + 1) * features]).astype(BF16)
            terms[h] = three_terms(low, factor, lane_group)
        cols[...] = dot_nt(transposed(w), normed_low).astype(BF16)
    key_wide = key_cols[...].astype(F32).reshape(HEADS, head_dim, keys)
    key_norm = jnp.max(jnp.sum(key_wide * key_wide, axis=1), axis=1, keepdims=True)

    bound = jnp.max(norm_ref[...] * key_norm) * scale**2

    sums_ref[...] = jnp.zeros_like(sums_ref)
    key_sums[...] = jnp.zeros_like(key_sums)
    value_sums[...] = jnp.zeros_like(value_sums)
    def fold(x):
        return jnp.sum(x.reshape(x.shape[0] // 8, 8, queries), axis=0)

    def operands(i, h):
        head = pl.ds(h * head_dim, head_dim)
        query, grad = q_cols[i, head, :], d_cols[i, head, :]
        return jnp.concatenate([query] * HEADS, axis=0), jnp.concatenate([grad] * HEADS, axis=0)

    def head_over_keys(h):
        head = pl.ds(h * head_dim, head_dim)
        rows = pl.ds(h * keys, keys)
        attn_low[head, :] = dot(value_cols[head, :], probs[rows, :]).astype(BF16)
        dq_low[head, :] = dot(key_cols[head, :], dscores[rows, :]).astype(BF16)

    def block_over_keys(i):
        dq = dq_low[...]
        sums_ref[pl.ds(2 * keys, features), :] += dot(dq, tokens_ref[i])
        sums_ref[pl.ds(2 * keys + features, features), :] += dot(attn_low[...], cot_ref[i])
        dq_ref[i] = dq.astype(F32).T.astype(BF16)

    def keys_over_queries(i, h):
        head = pl.ds(h * head_dim, head_dim)
        key_sums[head, :] += dot_nt(q_cols[i, head, :], dscores[pl.ds(h * keys, keys), :])

    def values_over_queries(i, h):
        head = pl.ds(h * head_dim, head_dim)
        value_sums[head, :] += dot_nt(d_cols[i, head, :], probs[pl.ds(h * keys, keys), :])

    def stage(i, h, sums, safe, only_first=False):
        following = (h + 1) % HEADS
        at = i if following else jnp.minimum(i + 1, blocks - 1)
        summed = jnp.maximum(i - 1, 0) if following else i
        query, grad = operands(at, following)
        slot, later = h % 2, following % 2
        if not only_first:
            total, delta = (jnp.sum(x, axis=0, keepdims=True) for x in sums)
            inverse = 1.0 / total
            delta = delta * inverse
        next_total = jnp.zeros((8, queries), F32)
        next_delta = jnp.zeros((8, queries), F32)
        if safe:
            scores = dot(key_terms[following], query)
            scores = scores - jnp.max(scores, axis=0, keepdims=True)
        for c in range(chunks):
            part = slice(c * KEY_CHUNK, (c + 1) * KEY_CHUNK)
            s = scores[part, :] if safe else dot(key_terms[following, part, :], query)
            dp = dot(value_terms[following, part, :], grad)
            if not only_first:
                if c == 0:
                    head_over_keys((h - 1) % HEADS)
                    keys_over_queries(summed, following)
                if c == chunks - 1:
                    values_over_queries(summed, following)
                    if h == 0:
                        block_over_keys(summed)
                rows = pl.ds(h * keys + c * KEY_CHUNK, KEY_CHUNK)
                p = exps[slot, part, :] * inverse
                probs[rows, :] = p.astype(BF16)
                dscores[rows, :] = (p * (dps[slot, part, :] - delta)).astype(BF16)
            e = jnp.exp(s)
            exps[later, part, :] = e
            dps[later, part, :] = dp
            next_total = next_total + fold(e)
            next_delta = next_delta + fold(e * dp)
        return next_total, next_delta

    def run(safe):
        def step(i, sums):
            for h in range(HEADS):
                sums = stage(i, h, sums, safe)
            return sums

        sums = stage(jnp.int32(-1), HEADS - 1, None, safe, only_first=True)
        lax.fori_loop(0, blocks, step, sums)

    for ref in (probs, dscores, attn_low, dq_low):
        ref[...] = jnp.zeros_like(ref)

    @pl.when(bound <= SAFE**2)
    def _():
        run(False)

    @pl.when(jnp.logical_not(bound <= SAFE**2))
    def _():
        run(True)

    head_over_keys(HEADS - 1)
    block_over_keys(blocks - 1)
    for h in range(1, HEADS):
        keys_over_queries(blocks - 1, h)
        values_over_queries(blocks - 1, h)

    sums_ref[pl.ds(0, keys), :] = key_sums[...].T
    sums_ref[pl.ds(keys, keys), :] = value_sums[...].T


def attend(tokens, cot, pool_sums, q_cols, d_cols, norm, w_key, w_value, gain, bias):
    blocks, queries, features = tokens.shape
    keys = pool_sums.shape[0]
    flops = 2 * blocks * queries * features * (6 * keys + 2 * features)
    vmem = pl.BlockSpec(memory_space=pltpu.VMEM)
    return pl.pallas_call(
        attend_kernel,
        name="attend",
        out_shape=(
            jax.ShapeDtypeStruct((2 * keys + 2 * features, features), F32),
            jax.ShapeDtypeStruct((blocks, queries, features), BF16),
        ),
        in_specs=[vmem] * 10,
        out_specs=(vmem, vmem),
        scratch_shapes=[
            pltpu.VMEM((HEADS, keys, features), BF16),
            pltpu.VMEM((HEADS, keys, features), BF16),
            pltpu.VMEM((features, keys), BF16),
            pltpu.VMEM((features, keys), BF16),
            pltpu.VMEM((2, keys, queries), F32),
            pltpu.VMEM((2, keys, queries), F32),
            pltpu.VMEM((HEADS * keys, queries), BF16),
            pltpu.VMEM((HEADS * keys, queries), BF16),
            pltpu.VMEM((features, keys), F32),
            pltpu.VMEM((features, keys), F32),
            pltpu.VMEM((features, queries), BF16),
            pltpu.VMEM((features, queries), BF16),
        ],
        cost_estimate=pl.CostEstimate(
            flops=flops,
            bytes_accessed=3 * tokens.size * 2,
            transcendentals=blocks * queries * keys * HEADS,
        ),
        compiler_params=pltpu.CompilerParams(vmem_limit_bytes=28 * 1024 * 1024),
    )(tokens, cot, pool_sums, q_cols, d_cols, norm, w_key, w_value, gain, bias)


def split_dot(low, wide):
    turned = low.astype(F32).T.astype(BF16)
    high = wide.astype(BF16)
    rest = wide - high.astype(F32)
    middle = rest.astype(BF16)
    last = (rest - middle.astype(F32)).astype(BF16)
    return dot(turned, high) + dot(turned, middle) + dot(turned, last)


def finish_kernel(
    grad_scale, sums_ref, pool_ref, dq_ref, w_query_ref, w_key_ref, w_value_ref, gain_ref,
    bias_ref, d_tokens_ref, d_query_ref, d_out_ref, d_key_ref, d_value_ref, d_gain_ref,
    d_bias_ref, pooled_grad_ref, own,
):
    keys, features = pool_ref.shape
    step = pl.program_id(0)
    cells_y, cells_x = 4, 8
    cells = cells_y * cells_x

    @pl.when(step == 0)
    def _():
        standard, inv_std = normalise(pool_ref[...])
        gain = gain_ref[...]
        normed_low = (standard * gain + bias_ref[...]).astype(BF16)
        key_grads = sums_ref[pl.ds(0, keys), :]
        value_grads = sums_ref[pl.ds(keys, keys), :]
        both = split_dot(normed_low, jnp.concatenate([key_grads, value_grads], 1)) * grad_scale
        d_key_ref[...] = both[:, :features]
        d_value_ref[...] = both[:, features:]
        d_normed = dot_nt(key_grads.astype(BF16), w_key_ref[...]) + dot_nt(
            value_grads.astype(BF16), w_value_ref[...]
        )
        d_gain_ref[...] = jnp.sum(d_normed * standard, axis=0, keepdims=True) * grad_scale
        d_bias_ref[...] = jnp.sum(d_normed, axis=0, keepdims=True) * grad_scale
        scaled = d_normed * gain
        d_pooled = inv_std * (
            scaled
            - jnp.mean(scaled, axis=1, keepdims=True)
            - standard * jnp.mean(scaled * standard, axis=1, keepdims=True)
        )
        pooled_grad_ref[...] = d_pooled * grad_scale
        own[...] = d_pooled * (1.0 / float(POOL**3))
        d_query_ref[...] = sums_ref[pl.ds(2 * keys, features), :].T * grad_scale
        d_out_ref[...] = sums_ref[pl.ds(2 * keys + features, features), :] * grad_scale

    rows = dq_ref.shape[0]
    plane_x = cells_x * POOL
    me = lax.axis_index("gz")
    offset = (me // (2 * POOL) * 2 + lax.rem(me, 2)) * cells
    cell_y = step * rows // (plane_x * POOL)
    mine = own[pl.ds(pl.multiple_of(offset + cell_y * cells_x, 8), cells_x), :]
    spread = jnp.concatenate(
        [jnp.broadcast_to(mine[x : x + 1, :], (POOL, features)) for x in range(cells_x)], axis=0
    )
    product = dot_nt(dq_ref[...], w_query_ref[...])
    summed = product.reshape(rows // plane_x, plane_x, features) + spread[None]
    d_tokens_ref[...] = summed.reshape(rows, features).astype(BF16)


def finish(sums, pool_sums, dq, w_query, w_key, w_value, gain, bias, grad_scale):
    keys, features = pool_sums.shape
    tokens = dq.shape[0]
    rows = 2048

    def whole(*shape):
        return pl.BlockSpec(shape, lambda i: (0,) * len(shape))

    square = whole(features, features)
    line = whole(1, features)
    tile = pl.BlockSpec((rows, features), lambda i: (i, 0))
    return pl.pallas_call(
        functools.partial(finish_kernel, grad_scale),
        name="finish",
        grid=(tokens // rows,),
        out_shape=(
            jax.ShapeDtypeStruct((tokens, features), BF16),
            *[jax.ShapeDtypeStruct((features, features), F32)] * 4,
            *[jax.ShapeDtypeStruct((1, features), F32)] * 2,
            jax.ShapeDtypeStruct((keys, features), F32),
        ),
        in_specs=[
            whole(*sums.shape), whole(keys, features), tile, square, square, square, line, line,
        ],
        out_specs=(tile, square, square, square, square, line, line, whole(keys, features)),
        scratch_shapes=[pltpu.VMEM((keys, features), F32)],
        compiler_params=pltpu.CompilerParams(vmem_limit_bytes=16 * 1024 * 1024),
    )(sums, pool_sums, dq, w_query, w_key, w_value, gain, bias)


def body(tokens, cotangent, w_query, w_key, w_value, w_out, ln_gain, ln_bias):
    devices = lax.axis_size("gz")
    _, rows_y, plane_x, features = tokens.shape
    slab_rows = rows_y * plane_x
    gain, bias = ln_gain.reshape(1, features), ln_bias.reshape(1, features)
    blocks = slab_rows // QUERIES
    pool_sums, token_rows, cot_rows, q_cols, d_cols, norm = exchange_pools(
        tokens.reshape(blocks, QUERIES, features),
        cotangent.reshape(blocks, QUERIES, features),
        jnp.concatenate([w_query, w_out], axis=0),
    )
    sums, dq = attend(
        token_rows, cot_rows, pool_sums, q_cols, d_cols, norm, w_key, w_value,
        gain, bias,
    )
    sums = sum_devices(sums)
    grad_scale = float(devices * slab_rows) ** (-0.5)
    d_tokens, d_query, d_out, d_key, d_value, d_gain, d_bias, pooled_grad = finish(
        sums, pool_sums, dq.reshape(slab_rows, features), w_query, w_key, w_value, gain, bias,
        grad_scale,
    )
    return (
        d_tokens.reshape(1, rows_y, plane_x, features),
        d_query,
        d_out,
        d_key,
        d_value,
        d_gain.reshape(features),
        d_bias.reshape(features),
        pooled_grad,
    )


def solution(mesh):
    in_specs = (P("gz", None, None, None), P("gz", None, None, None), P(), P(), P(), P(), P(), P())
    out_specs = (P("gz", None, None, None), P(), P(), P(), P(), P(), P(), P())
    return jax.shard_map(body, mesh=mesh, in_specs=in_specs, out_specs=out_specs, check_vma=False)
```

```python
import functools

import jax
import jax.numpy as jnp
from jax import lax
from jax.experimental import pallas as pl
from jax.experimental.pallas import tpu as pltpu
from jax.sharding import PartitionSpec as P

HEADS = 4
POOL = 16
EPSILON = 1e-05
MESH = pl.DeviceIdType.MESH
F32 = jnp.float32
BF16 = jnp.bfloat16

Z = 8
PLANE = 16
QUERIES = 512
KEY_CHUNK = 512
SAFE = 40.0


def dot(a, b):
    return lax.dot_general(a, b, (((1,), (0,)), ((), ())), preferred_element_type=F32)


def dot_nt(a, b):
    return lax.dot_general(a, b, (((1,), (1,)), ((), ())), preferred_element_type=F32)


def greet(partners):
    barrier = pltpu.get_barrier_semaphore()
    for partner in partners:
        pl.semaphore_signal(barrier, inc=1, device_id=(partner,), device_id_type=MESH)
    return lambda: pl.semaphore_wait(barrier, len(partners))


def send(src, dst, send_sem, recv_sem, partner):
    copy = pltpu.make_async_remote_copy(
        src_ref=src,
        dst_ref=dst,
        send_sem=send_sem,
        recv_sem=recv_sem,
        device_id=(partner,),
        device_id_type=MESH,
    )
    copy.start()
    return copy


LOADS = 4


def pool_kernel(
    tokens_hbm, cot_hbm, weights_ref, out_ref, tokens_ref, cot_ref, q_cols, d_cols, norm_ref, pieces, got, near, far, load_sem, sum_send, sum_recv, near_send,
    near_recv, far_send, far_recv,
):
    blocks, queries, features = tokens_ref.shape
    head_dim = features // HEADS
    plane_x = queries // 4
    cells_x = plane_x // POOL
    part = blocks // LOADS
    loads = [
        pltpu.make_async_copy(
            source.at[pl.ds(n * part, part)], target.at[pl.ds(n * part, part)],
            load_sem.at[k, n],
        )
        for k, (source, target) in enumerate(((tokens_hbm, tokens_ref), (cot_hbm, cot_ref)))
        for n in range(LOADS)
    ]
    for load in loads[:LOADS]:
        load.start()

    me = lax.axis_index("gz")
    core, chip = lax.rem(me, 2), me // 2
    member, block = lax.rem(chip, 16), chip // 16
    group = block * 2 + core
    members = [lax.rem(member + t, 16) for t in range(1, 16)]
    near_ids = [(block * 16 + other) * 2 + core for other in members]
    far_ids = []
    for t in range(1, 16):
        other = lax.rem(group + t, 16)
        far_ids.append(((other // 2) * 16 + member) * 2 + lax.rem(other, 2))
    await_partners = greet(near_ids + far_ids)

    share = got.shape[1]
    for y in range(LOADS):
        loads[y].wait()
        rows = jnp.zeros((plane_x, features), F32)
        for b in range(y * part, (y + 1) * part):
            wide = tokens_ref[b].astype(F32)
            for k in range(queries // plane_x):
                rows = rows + wide[k * plane_x : (k + 1) * plane_x, :]
        cells = jnp.sum(rows.reshape(cells_x, POOL, features), axis=1)
        for x in range(cells_x // share):
            pieces[y * (cells_x // share) + x] = cells[x * share : (x + 1) * share, :]
    for load in loads[LOADS:]:
        load.start()
    await_partners()
    copies = [
        send(pieces.at[members[t]], got.at[t], sum_send.at[t], sum_recv.at[t], near_ids[t])
        for t in range(15)
    ]

    w_query_t = transposed(weights_ref[:features, :])
    w_out = weights_ref[features:, :]

    def project_tokens(i, norm):
        cols = dot_nt(w_query_t, tokens_ref[i]).astype(BF16)
        q_cols[i] = cols
        wide = cols.astype(F32).reshape(HEADS, head_dim, queries)
        return jnp.maximum(norm, jnp.sum(wide * wide, axis=1))

    def project_grads(i, carry):
        d_cols[i] = dot_nt(w_out, cot_ref[i]).astype(BF16)
        return carry

    norm_ref[...] = lax.fori_loop(
        0, blocks, project_tokens, jnp.zeros((HEADS, queries), F32)
    )

    total = pieces[member]
    for t in range(15):
        copies[t].wait()
        total = total + got[t]
    near[member] = total
    copies = [
        send(near.at[member], near.at[member], near_send.at[t], near_recv.at[t], near_ids[t])
        for t in range(15)
    ]
    for load in loads[LOADS:]:
        load.wait()
    lax.fori_loop(0, blocks // 2, project_grads, 0)
    for copy in copies:
        copy.wait()
    for m in range(16):
        far[group, pl.ds(m * share, share), :] = near[m]

    copies = [
        send(far.at[group], far.at[group], far_send.at[t], far_recv.at[t], far_ids[t])
        for t in range(15)
    ]
    lax.fori_loop(blocks // 2, blocks, project_grads, 0)
    for copy in copies:
        copy.wait()
    for g in range(16):
        out_ref[pl.ds(g * 32, 32), :] = far[g]


def exchange_pools(tokens, cot, weights):
    blocks, queries, features = tokens.shape
    rows = 32
    dma = pltpu.SemaphoreType.DMA
    vmem = pl.BlockSpec(memory_space=pltpu.VMEM)
    hbm = pl.BlockSpec(memory_space=pl.ANY)
    by_rows = jax.ShapeDtypeStruct((blocks, queries, features), BF16)
    by_cols = jax.ShapeDtypeStruct((blocks, features, queries), BF16)
    return pl.pallas_call(
        pool_kernel,
        name="pool_exchange",
        out_shape=(
            jax.ShapeDtypeStruct((16 * rows, features), F32),
            by_rows, by_rows, by_cols, by_cols,
            jax.ShapeDtypeStruct((HEADS, queries), F32),
        ),
        in_specs=[hbm, hbm, vmem],
        out_specs=(vmem,) * 6,
        scratch_shapes=[
            pltpu.VMEM((16, rows // 16, features), F32),
            pltpu.VMEM((15, rows // 16, features), F32),
            pltpu.VMEM((16, rows // 16, features), F32),
            pltpu.VMEM((16, rows, features), F32),
            dma((2, LOADS)),
            *[dma((15,))] * 6,
        ],
        compiler_params=pltpu.CompilerParams(
            collective_id=0, has_side_effects=True, vmem_limit_bytes=44 * 1024 * 1024
        ),
    )(tokens, cot, weights)


STREAMS = ((0, 24), (24, 16))


def sum_kernel(
    w_ref, out_ref, got_half, half, got, along, full, pair_send, pair_recv, sum_send, sum_recv,
    z_send, z_recv, all_send, all_recv, back_send, back_recv,
):
    me = lax.axis_index("gz")
    core, chip = lax.rem(me, 2), me // 2
    z, plane = lax.rem(chip, Z), chip // Z
    sibling = me + 1 - 2 * core
    plane_members = [lax.rem(plane + t, PLANE) for t in range(1, PLANE)]
    plane_ids = [(other * Z + z) * 2 + core for other in plane_members]
    z_ids = [(plane * Z + lax.rem(z + t, Z)) * 2 + core for t in range(1, Z)]
    greet([sibling] + plane_ids + z_ids)()

    own = core * PLANE + plane
    mine = pl.ds(core * PLANE, PLANE)
    theirs = pl.ds((1 - core) * PLANE, PLANE)
    streams = range(len(STREAMS))
    rows = [pl.ds(*stream) for stream in STREAMS]

    pairs = [
        send(
            w_ref.at[theirs, rows[s]], got_half.at[:, rows[s]], pair_send.at[s], pair_recv.at[s],
            sibling,
        )
        for s in streams
    ]
    shares = []
    for s in streams:
        pairs[s].wait()
        half[:, rows[s], :] = w_ref[mine, rows[s], :] + got_half[:, rows[s], :]
        shares.append(
            [
                send(
                    half.at[plane_members[t], rows[s]], got.at[t, rows[s]], sum_send.at[s, t],
                    sum_recv.at[s, t], plane_ids[t],
                )
                for t in range(PLANE - 1)
            ]
        )
    lines = []
    for s in streams:
        total = half[plane, rows[s], :]
        for t in range(PLANE - 1):
            shares[s][t].wait()
            total = total + got[t, rows[s], :]
        along[z, rows[s], :] = total
        lines.append(
            [
                send(
                    along.at[z, rows[s]], along.at[z, rows[s]], z_send.at[s, t], z_recv.at[s, t],
                    z_ids[t],
                )
                for t in range(Z - 1)
            ]
        )
    gathers = []
    for s in streams:
        for copy in lines[s]:
            copy.wait()
        total = along[0, rows[s], :]
        for k in range(1, Z):
            total = total + along[k, rows[s], :]
        full[own, rows[s], :] = total
        gathers.append(
            [
                send(
                    full.at[own, rows[s]], full.at[own, rows[s]], all_send.at[s, t],
                    all_recv.at[s, t], plane_ids[t],
                )
                for t in range(PLANE - 1)
            ]
        )
    backs = []
    for s in streams:
        for copy in gathers[s]:
            copy.wait()
        backs.append(
            send(
                full.at[mine, rows[s]], full.at[mine, rows[s]], back_send.at[s], back_recv.at[s],
                sibling,
            )
        )
    for copy in backs:
        copy.wait()
    out_ref[...] = full[...]


def sum_devices(w):
    rows, features = w.shape
    share = rows // 2 // PLANE
    count = len(STREAMS)
    dma = pltpu.SemaphoreType.DMA
    return pl.pallas_call(
        sum_kernel,
        name="sum_devices",
        out_shape=jax.ShapeDtypeStruct((2 * PLANE, share, features), F32),
        in_specs=[pl.BlockSpec(memory_space=pltpu.VMEM)],
        out_specs=pl.BlockSpec(memory_space=pltpu.VMEM),
        scratch_shapes=[
            pltpu.VMEM((PLANE, share, features), F32),
            pltpu.VMEM((PLANE, share, features), F32),
            pltpu.VMEM((PLANE - 1, share, features), F32),
            pltpu.VMEM((Z, share, features), F32),
            pltpu.VMEM((2 * PLANE, share, features), F32),
            dma((count,)),
            dma((count,)),
            dma((count, PLANE - 1)),
            dma((count, PLANE - 1)),
            dma((count, Z - 1)),
            dma((count, Z - 1)),
            dma((count, PLANE - 1)),
            dma((count, PLANE - 1)),
            dma((count,)),
            dma((count,)),
        ],
        compiler_params=pltpu.CompilerParams(
            collective_id=1, has_side_effects=True, vmem_limit_bytes=10 * 1024 * 1024
        ),
    )(w.reshape(2 * PLANE, share, features)).reshape(rows, features)


def normalise(pool_sums):
    pooled = pool_sums * (1.0 / float(POOL**3))
    mean = jnp.mean(pooled, axis=1, keepdims=True)
    centered = pooled - mean
    var = jnp.mean(centered * centered, axis=1, keepdims=True)
    inv_std = lax.rsqrt(var + EPSILON)
    return centered * inv_std, inv_std


def transposed(w):
    return w.astype(F32).T.astype(BF16)


def three_terms(low, factor, lane_group):
    wide = low.astype(F32) * factor
    high = wide.astype(BF16)
    rest = wide - high.astype(F32)
    middle = rest.astype(BF16)
    last = (rest - middle.astype(F32)).astype(BF16)
    zero = jnp.zeros_like(high)
    return jnp.where(
        lane_group == 0,
        high,
        jnp.where(lane_group == 1, middle, jnp.where(lane_group == 2, last, zero)),
    )


def attend_kernel(
    tokens_ref, cot_ref, pool_ref, q_cols, d_cols, norm_ref, w_key_ref,
    w_value_ref, gain_ref, bias_ref, sums_ref, dq_ref, key_terms, value_terms, key_cols,
    value_cols, exps, dps, probs, dscores, key_sums, value_sums, attn_low, dq_low,
):
    blocks, queries, features = tokens_ref.shape
    keys = pool_ref.shape[0]
    head_dim = features // HEADS
    scale = head_dim ** (-0.5)
    chunks = keys // KEY_CHUNK

    standard, _ = normalise(pool_ref[...])
    normed_low = (standard * gain_ref[...] + bias_ref[...]).astype(BF16)
    source = lax.broadcasted_iota(jnp.int32, (features, HEADS * features), 0)
    target = lax.broadcasted_iota(jnp.int32, (features, HEADS * features), 1)
    spread = jnp.where(
        source == (target // features) * head_dim + lax.rem(target, head_dim), 1.0, 0.0
    ).astype(BF16)
    lane = lax.broadcasted_iota(jnp.int32, (keys, features), 1)
    lane_group = lane // head_dim
    for w_ref, factor, terms, cols in (
        (w_key_ref, scale, key_terms, key_cols),
        (w_value_ref, scale, value_terms, value_cols),
    ):
        w = w_ref[...]
        wide_w = dot(w, spread).astype(BF16)
        for h in range(HEADS):
            low = dot(normed_low, wide_w[:, h * features : (h + 1) * features]).astype(BF16)
            terms[h] = three_terms(low, factor, lane_group)
        cols[...] = dot_nt(transposed(w), normed_low).astype(BF16)
    key_wide = key_cols[...].astype(F32).reshape(HEADS, head_dim, keys)
    key_norm = jnp.max(jnp.sum(key_wide * key_wide, axis=1), axis=1, keepdims=True)

    bound = jnp.max(norm_ref[...] * key_norm) * scale**2

    sums_ref[...] = jnp.zeros_like(sums_ref)
    key_sums[...] = jnp.zeros_like(key_sums)
    value_sums[...] = jnp.zeros_like(value_sums)
    def fold(x):
        return jnp.sum(x.reshape(x.shape[0] // 8, 8, queries), axis=0)

    def operands(i, h):
        head = pl.ds(h * head_dim, head_dim)
        query, grad = q_cols[i, head, :], d_cols[i, head, :]
        return jnp.concatenate([query] * HEADS, axis=0), jnp.concatenate([grad] * HEADS, axis=0)

    def head_over_keys(h):
        head = pl.ds(h * head_dim, head_dim)
        rows = pl.ds(h * keys, keys)
        attn_low[head, :] = dot(value_cols[head, :], probs[rows, :]).astype(BF16)
        dq_low[head, :] = dot(key_cols[head, :], dscores[rows, :]).astype(BF16)

    def block_over_keys(i):
        dq = dq_low[...]
        sums_ref[pl.ds(2 * keys, features), :] += dot(dq, tokens_ref[i])
        sums_ref[pl.ds(2 * keys + features, features), :] += dot(attn_low[...], cot_ref[i])
        dq_ref[i] = dq.astype(F32).T.astype(BF16)

    def keys_over_queries(i, h):
        head = pl.ds(h * head_dim, head_dim)
        key_sums[head, :] += dot_nt(q_cols[i, head, :], dscores[pl.ds(h * keys, keys), :])

    def values_over_queries(i, h):
        head = pl.ds(h * head_dim, head_dim)
        value_sums[head, :] += dot_nt(d_cols[i, head, :], probs[pl.ds(h * keys, keys), :])

    def stage(i, h, sums, safe, only_first=False):
        following = (h + 1) % HEADS
        at = i if following else jnp.minimum(i + 1, blocks - 1)
        summed = jnp.maximum(i - 1, 0) if following else i
        query, grad = operands(at, following)
        slot, later = h % 2, following % 2
        if not only_first:
            total, delta = (jnp.sum(x, axis=0, keepdims=True) for x in sums)
            inverse = 1.0 / total
            delta = delta * inverse
        next_total = jnp.zeros((8, queries), F32)
        next_delta = jnp.zeros((8, queries), F32)
        if safe:
            scores = dot(key_terms[following], query)
            scores = scores - jnp.max(scores, axis=0, keepdims=True)
        for c in range(chunks):
            part = slice(c * KEY_CHUNK, (c + 1) * KEY_CHUNK)
            s = scores[part, :] if safe else dot(key_terms[following, part, :], query)
            dp = dot(value_terms[following, part, :], grad)
            if not only_first:
                if c == 0:
                    head_over_keys((h - 1) % HEADS)
                    keys_over_queries(summed, following)
                if c == chunks - 1:
                    values_over_queries(summed, following)
                    if h == 0:
                        block_over_keys(summed)
                rows = pl.ds(h * keys + c * KEY_CHUNK, KEY_CHUNK)
                p = exps[slot, part, :] * inverse
                probs[rows, :] = p.astype(BF16)
                dscores[rows, :] = (p * (dps[slot, part, :] - delta)).astype(BF16)
            e = jnp.exp(s)
            exps[later, part, :] = e
            dps[later, part, :] = dp
            next_total = next_total + fold(e)
            next_delta = next_delta + fold(e * dp)
        return next_total, next_delta

    def run(safe):
        def step(i, sums):
            for h in range(HEADS):
                sums = stage(i, h, sums, safe)
            return sums

        sums = stage(jnp.int32(-1), HEADS - 1, None, safe, only_first=True)
        lax.fori_loop(0, blocks, step, sums)

    for ref in (probs, dscores, attn_low, dq_low):
        ref[...] = jnp.zeros_like(ref)

    @pl.when(bound <= SAFE**2)
    def _():
        run(False)

    @pl.when(jnp.logical_not(bound <= SAFE**2))
    def _():
        run(True)

    head_over_keys(HEADS - 1)
    block_over_keys(blocks - 1)
    for h in range(1, HEADS):
        keys_over_queries(blocks - 1, h)
        values_over_queries(blocks - 1, h)

    sums_ref[pl.ds(0, keys), :] = key_sums[...].T
    sums_ref[pl.ds(keys, keys), :] = value_sums[...].T


def attend(tokens, cot, pool_sums, q_cols, d_cols, norm, w_key, w_value, gain, bias):
    blocks, queries, features = tokens.shape
    keys = pool_sums.shape[0]
    flops = 2 * blocks * queries * features * (6 * keys + 2 * features)
    vmem = pl.BlockSpec(memory_space=pltpu.VMEM)
    return pl.pallas_call(
        attend_kernel,
        name="attend",
        out_shape=(
            jax.ShapeDtypeStruct((2 * keys + 2 * features, features), F32),
            jax.ShapeDtypeStruct((blocks, queries, features), BF16),
        ),
        in_specs=[vmem] * 10,
        out_specs=(vmem, vmem),
        scratch_shapes=[
            pltpu.VMEM((HEADS, keys, features), BF16),
            pltpu.VMEM((HEADS, keys, features), BF16),
            pltpu.VMEM((features, keys), BF16),
            pltpu.VMEM((features, keys), BF16),
            pltpu.VMEM((2, keys, queries), F32),
            pltpu.VMEM((2, keys, queries), F32),
            pltpu.VMEM((HEADS * keys, queries), BF16),
            pltpu.VMEM((HEADS * keys, queries), BF16),
            pltpu.VMEM((features, keys), F32),
            pltpu.VMEM((features, keys), F32),
            pltpu.VMEM((features, queries), BF16),
            pltpu.VMEM((features, queries), BF16),
        ],
        cost_estimate=pl.CostEstimate(
            flops=flops,
            bytes_accessed=3 * tokens.size * 2,
            transcendentals=blocks * queries * keys * HEADS,
        ),
        compiler_params=pltpu.CompilerParams(vmem_limit_bytes=28 * 1024 * 1024),
    )(tokens, cot, pool_sums, q_cols, d_cols, norm, w_key, w_value, gain, bias)


def split_dot(low, wide):
    turned = low.astype(F32).T.astype(BF16)
    high = wide.astype(BF16)
    rest = wide - high.astype(F32)
    middle = rest.astype(BF16)
    last = (rest - middle.astype(F32)).astype(BF16)
    return dot(turned, high) + dot(turned, middle) + dot(turned, last)


def finish_kernel(
    grad_scale, sums_ref, pool_ref, dq_ref, w_query_ref, w_key_ref, w_value_ref, gain_ref,
    bias_ref, d_tokens_ref, d_query_ref, d_out_ref, d_key_ref, d_value_ref, d_gain_ref,
    d_bias_ref, pooled_grad_ref, own,
):
    keys, features = pool_ref.shape
    step = pl.program_id(0)
    cells_y, cells_x = 4, 8
    cells = cells_y * cells_x

    @pl.when(step == 0)
    def _():
        standard, inv_std = normalise(pool_ref[...])
        gain = gain_ref[...]
        normed_low = (standard * gain + bias_ref[...]).astype(BF16)
        key_grads = sums_ref[pl.ds(0, keys), :]
        value_grads = sums_ref[pl.ds(keys, keys), :]
        both = split_dot(normed_low, jnp.concatenate([key_grads, value_grads], 1)) * grad_scale
        d_key_ref[...] = both[:, :features]
        d_value_ref[...] = both[:, features:]
        d_normed = dot_nt(key_grads.astype(BF16), w_key_ref[...]) + dot_nt(
            value_grads.astype(BF16), w_value_ref[...]
        )
        d_gain_ref[...] = jnp.sum(d_normed * standard, axis=0, keepdims=True) * grad_scale
        d_bias_ref[...] = jnp.sum(d_normed, axis=0, keepdims=True) * grad_scale
        scaled = d_normed * gain
        d_pooled = inv_std * (
            scaled
            - jnp.mean(scaled, axis=1, keepdims=True)
            - standard * jnp.mean(scaled * standard, axis=1, keepdims=True)
        )
        pooled_grad_ref[...] = d_pooled * grad_scale
        own[...] = d_pooled * (1.0 / float(POOL**3))
        d_query_ref[...] = sums_ref[pl.ds(2 * keys, features), :].T * grad_scale
        d_out_ref[...] = sums_ref[pl.ds(2 * keys + features, features), :] * grad_scale

    rows = dq_ref.shape[0]
    plane_x = cells_x * POOL
    me = lax.axis_index("gz")
    offset = (me // (2 * POOL) * 2 + lax.rem(me, 2)) * cells
    cell_y = step * rows // (plane_x * POOL)
    mine = own[pl.ds(pl.multiple_of(offset + cell_y * cells_x, 8), cells_x), :]
    spread = jnp.concatenate(
        [jnp.broadcast_to(mine[x : x + 1, :], (POOL, features)) for x in range(cells_x)], axis=0
    )
    product = dot_nt(dq_ref[...], w_query_ref[...])
    summed = product.reshape(rows // plane_x, plane_x, features) + spread[None]
    d_tokens_ref[...] = summed.reshape(rows, features).astype(BF16)


def finish(sums, pool_sums, dq, w_query, w_key, w_value, gain, bias, grad_scale):
    keys, features = pool_sums.shape
    tokens = dq.shape[0]
    rows = 2048

    def whole(*shape):
        return pl.BlockSpec(shape, lambda i: (0,) * len(shape))

    square = whole(features, features)
    line = whole(1, features)
    tile = pl.BlockSpec((rows, features), lambda i: (i, 0))
    return pl.pallas_call(
        functools.partial(finish_kernel, grad_scale),
        name="finish",
        grid=(tokens // rows,),
        out_shape=(
            jax.ShapeDtypeStruct((tokens, features), BF16),
            *[jax.ShapeDtypeStruct((features, features), F32)] * 4,
            *[jax.ShapeDtypeStruct((1, features), F32)] * 2,
            jax.ShapeDtypeStruct((keys, features), F32),
        ),
        in_specs=[
            whole(*sums.shape), whole(keys, features), tile, square, square, square, line, line,
        ],
        out_specs=(tile, square, square, square, square, line, line, whole(keys, features)),
        scratch_shapes=[pltpu.VMEM((keys, features), F32)],
        compiler_params=pltpu.CompilerParams(vmem_limit_bytes=16 * 1024 * 1024),
    )(sums, pool_sums, dq, w_query, w_key, w_value, gain, bias)


def body(tokens, cotangent, w_query, w_key, w_value, w_out, ln_gain, ln_bias):
    devices = lax.axis_size("gz")
    _, rows_y, plane_x, features = tokens.shape
    slab_rows = rows_y * plane_x
    gain, bias = ln_gain.reshape(1, features), ln_bias.reshape(1, features)
    blocks = slab_rows // QUERIES
    pool_sums, token_rows, cot_rows, q_cols, d_cols, norm = exchange_pools(
        tokens.reshape(blocks, QUERIES, features),
        cotangent.reshape(blocks, QUERIES, features),
        jnp.concatenate([w_query, w_out], axis=0),
    )
    sums, dq = attend(
        token_rows, cot_rows, pool_sums, q_cols, d_cols, norm, w_key, w_value,
        gain, bias,
    )
    sums = sum_devices(sums)
    grad_scale = float(devices * slab_rows) ** (-0.5)
    d_tokens, d_query, d_out, d_key, d_value, d_gain, d_bias, pooled_grad = finish(
        sums, pool_sums, dq.reshape(slab_rows, features), w_query, w_key, w_value, gain, bias,
        grad_scale,
    )
    return (
        d_tokens.reshape(1, rows_y, plane_x, features),
        d_query,
        d_out,
        d_key,
        d_value,
        d_gain.reshape(features),
        d_bias.reshape(features),
        pooled_grad,
    )


def solution(mesh):
    in_specs = (P("gz", None, None, None), P("gz", None, None, None), P(), P(), P(), P(), P(), P())
    out_specs = (P("gz", None, None, None), P(), P(), P(), P(), P(), P(), P())
    return jax.shard_map(body, mesh=mesh, in_specs=in_specs, out_specs=out_specs, check_vma=False)
```
